256 devices in a mesh: dp: 8 (over z), seq: 32 (over y, x, core).
Axes of the slice: x: 4, y: 4, z: 8, core: 2. Of those that a mesh axis runs over, the one named last changes fastest.
Arguments:
- events: bfloat16 [8, 32, 256, 1024], P('dp', 'seq'), may hold values from -6 to 6
- lengths: int32 [8, 4], P('dp'), may hold values from 1 to 32, 64 in all within a row
- weight_in: bfloat16 [1024, 4096], replicated, may hold values from -0.1875 to 0.1875
- weight_out: bfloat16 [1024, 1024], replicated, may hold values from -0.1875 to 0.1875
- cotangent: bfloat16 [8, 32, 256, 1024], P('dp', 'seq'), may hold values from -6 to 6
Outputs:
- layer_out: bfloat16 [8, 32, 256, 1024], P('dp', 'seq')
- event_grads: bfloat16 [8, 32, 256, 1024], P('dp', 'seq')
- weight_key_grad: float32 [1024, 1024], P(('dp', 'seq'))
The draws below stay inside these ranges and needn't reach their ends.
Inputs may be any that keep to these rules, and one draw needn't show every extreme that they name: lengths[g, u] counts tiles of 128 events; each group's lengths sum to 64 and one of them equals 32.
All inputs are finite; a program needn't handle non-finite values.
Results may differ from the reference program's by a relative error of at most 0.015.
Values may be sent and summed in bfloat16 or wider, within the bound.
No kernel may reach another device: no remote copies, remote signals or barrier semaphores. Data moves between devices by JAX's collectives and lax.ppermute only.
A program may use at most 128 MiB of HBM per device.

```python
import math
import jax
import jax.numpy as jnp
import numpy as np
from jax import lax

D = 1024
HEADS = 8
HEAD = 128
TILE = 128
MOST = 4
USERS = 4
GROUPS = 8
PAIRS = 32
TILES = 64
LONGEST = 32


def steps_of(rng, shape, shards, low, largest):
    level = 1.0
    for dim, shards_of in shards:
        draws = jax.random.uniform(jax.random.fold_in(jax.random.fold_in(rng, 6), dim), (shards_of,), jnp.float32, low / len(shards), largest / len(shards))
        level = level * jnp.repeat(jnp.exp(draws), shape[dim] // shards_of).reshape((-1,) + (1,) * (len(shape) - 1 - dim))
    return level


def profile(amount, total, limit, skew):
    weights = [(1 << 20) // math.isqrt(rank ** skew) + 1 for rank in range(2, amount + 1)]
    spare, holding = total - limit - (amount - 1), [1] * (amount - 1)
    while spare > 0:
        candidates = [i for i in range(amount - 1) if holding[i] < limit]
        whole, remaining = sum([weights[i] for i in candidates]), spare
        for i in candidates:
            extra = min(limit - holding[i], max(1, remaining * weights[i] // whole), spare)
            holding[i] = holding[i] + extra
            spare = spare - extra
    return np.array([limit] + holding)


def uneven(key, count, total, bound, slope):
    if count == 2:
        one = jax.random.randint(key, (), max(1, total - bound), min(bound, total - 1) + 1)
        return jnp.stack([one, total - one])
    tallies = jnp.asarray(profile(count, total, bound, slope), jnp.int32)
    twos = (count - 1) // 2
    source_of, receiver = tallies[1:1 + 2 * twos:2], tallies[2:2 + 2 * twos:2]
    margin = jnp.minimum(source_of - 1, bound - receiver)
    shifted = jax.random.randint(jax.random.fold_in(key, 1), (twos,), 0, 1 << 20) % (margin + 1)
    tallies = tallies.at[1:1 + 2 * twos:2].set(source_of - shifted).at[2:2 + 2 * twos:2].set(receiver + shifted)
    return tallies[jax.random.permutation(jax.random.fold_in(key, 2), count)]


def normal_values(key, shape, deviation, reach, cuts=(), kind=jnp.bfloat16):
    array = jax.random.normal(key, shape, jnp.float32) * deviation
    if len(cuts) > 0:
        array = steps_of(key, shape, cuts, -0.22, 0.18) * array
    return jnp.clip(array, min=-reach, max=reach).astype(kind)


def setup_inputs(seed: int = 0) -> dict:
    key_list = jax.random.split(jax.random.key(seed), 6)
    events = normal_values(key_list[0], (GROUPS, PAIRS, 2 * TILE, D), 1.0, 6.0, ((0, 8), (1, 32)))
    lengths = jax.vmap(lambda own: uneven(own, USERS, TILES, LONGEST, 2))(jax.random.split(key_list[1], GROUPS)).reshape((GROUPS, USERS)).astype(jnp.int32)
    weight_in = normal_values(key_list[2], (D, 4 * D), D ** -0.5, 0.1875)
    weight_out = normal_values(key_list[3], (D, D), D ** -0.5, 0.1875)
    cotangent = normal_values(key_list[4], (GROUPS, PAIRS, 2 * TILE, D), 1.0, 6.0, ((0, 8), (1, 32)))
    return dict(events=events, lengths=lengths, weight_in=weight_in, weight_out=weight_out, cotangent=cotangent)


EPSILON = 1e-06

def layer_norm(values):
    centre = lax.optimization_barrier(jnp.mean(values, axis=-1, keepdims=True))
    centred = values - centre
    spread = lax.optimization_barrier(jnp.mean(centred * centred, axis=-1, keepdims=True))
    recip = lax.rsqrt(spread + EPSILON)
    return (centred * recip, recip)

def norm_back(upstream, normed_f, recip):
    first = lax.optimization_barrier(jnp.mean(upstream, axis=-1, keepdims=True))
    second = lax.optimization_barrier(jnp.mean(upstream * normed_f, axis=-1, keepdims=True))
    return recip * (upstream - first - normed_f * second)

def silu_slope(values):
    sigmoid = jax.nn.sigmoid(values)
    return sigmoid * (1.0 + values * (1.0 - sigmoid))

def round_half(values):
    return lax.optimization_barrier(values.astype(jnp.bfloat16)).astype(jnp.float32)

def to_sequence(block):
    lower = block[:, :TILE]
    upper = block[::-1, TILE:]
    return jnp.concatenate([lower, upper], axis=0).reshape(TILES * TILE, block.shape[-1])

def from_sequence(ordered):
    tiles = ordered.reshape(TILES, TILE, ordered.shape[-1])
    return jnp.concatenate([tiles[:PAIRS], tiles[PAIRS:][::-1]], axis=1)

def tile_history(tile_pos, history_ends):
    return lax.optimization_barrier(jnp.sum((tile_pos[..., None] >= history_ends).astype(jnp.int32), axis=-1))

def tile_scale(history, group_lengths):
    labels = jnp.arange(group_lengths.shape[0], dtype=jnp.int32)
    picked = lax.optimization_barrier(jnp.sum(jnp.where(history[..., None] == labels, group_lengths, 0), axis=-1))
    return 1.0 / (picked * TILE).astype(jnp.float32)

def group_pass(block, group_lengths, back_block, weight_in, weight_out):
    model_width = block.shape[-1]
    scale = HEAD ** (-0.5)
    history_ends = jnp.cumsum(group_lengths).astype(jnp.int32)
    events_f = to_sequence(block).astype(jnp.float32)
    normed_f, recip = layer_norm(events_f)
    normed = normed_f.astype(jnp.bfloat16)
    pre_act = jnp.dot(normed, weight_in, preferred_element_type=jnp.float32)
    projected = jax.nn.silu(pre_act).astype(jnp.bfloat16)
    gate_part = projected[:, :model_width]
    value_part = projected[:, model_width:2 * model_width]
    query_part = projected[:, 2 * model_width:3 * model_width]
    key_part = projected[:, 3 * model_width:]
    pad_rows = jnp.zeros(((MOST - 1) * TILE, model_width), jnp.bfloat16)
    key_padded = jnp.concatenate([pad_rows, key_part], axis=0)
    value_padded = jnp.concatenate([pad_rows, value_part], axis=0)
    window_ids = jnp.arange(MOST * TILE, dtype=jnp.int32)
    row_ids = jnp.arange(TILE, dtype=jnp.int32)

    def tile_terms(tile_pos):
        first = (tile_pos * TILE).astype(jnp.int32)
        queries = lax.dynamic_slice_in_dim(query_part, first, TILE, 0).reshape(TILE, HEADS, HEAD).astype(jnp.float32)
        keys = lax.dynamic_slice_in_dim(key_padded, first, MOST * TILE, 0).reshape(MOST * TILE, HEADS, HEAD).astype(jnp.float32)
        values = lax.dynamic_slice_in_dim(value_padded, first, MOST * TILE, 0).reshape(MOST * TILE, HEADS, HEAD).astype(jnp.float32)
        scores = jnp.einsum('rhd,chd->hrc', queries, keys) * scale
        key_tile = tile_pos - (MOST - 1) + window_ids // TILE
        key_row = key_tile * TILE + window_ids % TILE
        query_row = tile_pos * TILE + row_ids
        own = tile_history(tile_pos, history_ends)
        same = tile_history(jnp.maximum(key_tile, 0), history_ends) == own
        live = (key_tile >= 0) & same
        live = live[None, None, :] & (key_row[None, None, :] <= query_row[None, :, None])
        inverse = tile_scale(own, group_lengths)
        return (first, queries, keys, values, scores, live, inverse)

    def forward_tile(tile_pos):
        first, queries, keys, values, scores, live, inverse = tile_terms(tile_pos)
        attention = round_half(jnp.where(live, jax.nn.silu(scores), 0.0) * inverse)
        return jnp.einsum('hrc,chd->rhd', attention, values).reshape(TILE, model_width)
    tile_list = jnp.arange(TILES, dtype=jnp.int32)
    attended = lax.map(forward_tile, tile_list).reshape(TILES * TILE, model_width)
    attended_n, attended_recip = layer_norm(attended)
    gated = (attended_n * gate_part.astype(jnp.float32)).astype(jnp.bfloat16)
    layer_out = (events_f + jnp.dot(gated, weight_out, preferred_element_type=jnp.float32)).astype(jnp.bfloat16)
    back = to_sequence(back_block)
    d_gated = jnp.dot(back, weight_out.T, preferred_element_type=jnp.float32)
    d_gate = d_gated * attended_n
    d_attended = norm_back(d_gated * gate_part.astype(jnp.float32), attended_n, attended_recip).astype(jnp.bfloat16)

    def backward_tile(padded_grads, tile_pos):
        first, queries, keys, values, scores, live, inverse = tile_terms(tile_pos)
        attention = round_half(jnp.where(live, jax.nn.silu(scores), 0.0) * inverse)
        upstream = lax.dynamic_slice_in_dim(d_attended, first, TILE, 0).reshape(TILE, HEADS, HEAD).astype(jnp.float32)
        d_weights = jnp.einsum('rhd,chd->hrc', upstream, values)
        d_scores = round_half(jnp.where(live, d_weights * silu_slope(scores), 0.0) * inverse)
        d_query = jnp.einsum('hrc,chd->rhd', d_scores, keys) * scale
        d_key = jnp.einsum('hrc,rhd->chd', d_scores, queries) * scale
        d_value = jnp.einsum('hrc,rhd->chd', attention, upstream)
        window = jnp.concatenate([d_key.reshape(MOST * TILE, model_width), d_value.reshape(MOST * TILE, model_width)], axis=1)
        current = lax.dynamic_slice_in_dim(padded_grads, first, MOST * TILE, 0)
        padded_grads = lax.dynamic_update_slice_in_dim(padded_grads, current + window, first, 0)
        return (padded_grads, d_query.reshape(TILE, model_width))
    start_grads = jnp.zeros(((TILES + MOST - 1) * TILE, 2 * model_width), jnp.float32)
    padded_grads, d_query_all = lax.scan(backward_tile, start_grads, tile_list)
    d_query_all = d_query_all.reshape(TILES * TILE, model_width)
    d_key_all = padded_grads[(MOST - 1) * TILE:, :model_width]
    d_value_all = padded_grads[(MOST - 1) * TILE:, model_width:]
    d_pre = (jnp.concatenate([d_gate, d_value_all, d_query_all, d_key_all], axis=1) * silu_slope(pre_act)).astype(jnp.bfloat16)
    d_normed = jnp.dot(d_pre, weight_in.T, preferred_element_type=jnp.float32)
    event_grads = (back.astype(jnp.float32) + norm_back(d_normed, normed_f, recip)).astype(jnp.bfloat16)
    grad_key = jnp.dot(normed.T, d_pre[:, 3 * model_width:], preferred_element_type=jnp.float32)
    return (from_sequence(layer_out), from_sequence(event_grads), grad_key)

def reference(events, lengths, weight_in, weight_out, cotangent):

    def one_group(items):
        block, group_lengths, back_block = items
        return group_pass(block, group_lengths, back_block, weight_in, weight_out)
    layer_out, event_grads, grad_key = lax.map(one_group, (events, lengths, cotangent))
    return (layer_out, event_grads, lax.optimization_barrier(jnp.sum(grad_key, axis=0)))
```

```python
import jax
import jax.numpy as jnp
from jax import lax
from jax.experimental import pallas as pl
from jax.experimental.pallas import tpu as pltpu
from jax.sharding import Mesh, PartitionSpec as P

HEADS = 8
HEAD = 128
TILE = 128
MOST = 4
EPSILON = 1e-06
SCALE = HEAD ** (-0.5)
SEQ = ("y", "x", "core")
MIB = 1024 * 1024

F32 = jnp.float32
BF16 = jnp.bfloat16


def chain_device(block, chips):
    return 2 * block if block < chips else 2 * (2 * chips - 1 - block) + 1


def tile_owner(tile, pairs):
    return tile if tile < pairs else 2 * pairs - 1 - tile


def routes(pairs):
    chips = pairs // 2
    place = [chain_device(block, chips) for block in range(pairs)]
    near_odd = [(tile_owner(2 * b - 1, pairs), place[b]) for b in range(1, pairs)]
    near_even = [(tile_owner(2 * b - 2, pairs), place[b]) for b in range(1, pairs)]
    onward = [(place[b - 1], place[b]) for b in range(2, pairs)]
    far_odd = [(tile_owner(2 * b - 3, pairs), place[b]) for b in range(2, pairs)]
    return near_odd, near_even, onward, far_odd


def reverse(route):
    return [(b, a) for a, b in route]


def move(block, route):
    return lax.ppermute(block, SEQ, route)


def normalize(values):
    centre = jnp.mean(values, axis=-1, keepdims=True)
    centred = values - centre
    spread = jnp.mean(centred * centred, axis=-1, keepdims=True)
    recip = lax.rsqrt(spread + EPSILON)
    return centred * recip, recip


def norm_back(upstream, normed_f, recip):
    first = jnp.mean(upstream, axis=-1, keepdims=True)
    second = jnp.mean(upstream * normed_f, axis=-1, keepdims=True)
    return recip * (upstream - first - normed_f * second)


def silu_pair(half):
    bend = jnp.tanh(half)
    silu = half + half * bend
    sigmoid = 0.5 + 0.5 * bend
    return silu, sigmoid + silu * (1.0 - sigmoid)


def dot_nn(left, right):
    return lax.dot_general(left, right, (((1,), (0,)), ((), ())), preferred_element_type=F32)


def dot_nt(left, right):
    return lax.dot_general(left, right, (((1,), (1,)), ((), ())), preferred_element_type=F32)


def dot_tn(left, right):
    return lax.dot_general(left, right, (((0,), (0,)), ((), ())), preferred_element_type=F32)


def whole():
    return pl.BlockSpec(memory_space=pltpu.VMEM)


def project_kernel(*refs):
    tiles, (weight, normed, proj, slope) = refs[:-4], refs[-4:]

    @pl.when(pl.program_id(0) == 0)
    def _():
        for n, tile in enumerate(tiles):
            rows = tile.shape[0]
            normed[n * rows : (n + 1) * rows, :] = normalize(tile[...].astype(F32))[0].astype(BF16)

    pre = dot_nn(normed[...], weight[...])
    silu, bent = silu_pair(0.5 * pre)
    proj[...] = silu.astype(BF16)
    slope[...] = bent.astype(BF16)


def project(tiles, weight, columns, pick):
    rows = sum(t.shape[0] for t in tiles)
    width = tiles[0].shape[1]
    step = 512
    return pl.pallas_call(
        project_kernel,
        grid=(columns // step,),
        in_specs=[pl.BlockSpec(t.shape, lambda i: (0, 0)) for t in tiles]
        + [pl.BlockSpec((width, step), lambda i: (0, pick(i)))],
        out_specs=[
            pl.BlockSpec((rows, width), lambda i: (0, 0)),
            pl.BlockSpec((rows, step), lambda i: (0, i)),
            pl.BlockSpec((rows, step), lambda i: (0, i)),
        ],
        out_shape=[
            jax.ShapeDtypeStruct((rows, width), BF16),
            jax.ShapeDtypeStruct((rows, columns), BF16),
            jax.ShapeDtypeStruct((rows, columns), BF16),
        ],
        compiler_params=pltpu.CompilerParams(vmem_limit_bytes=40 * MIB),
        cost_estimate=pl.CostEstimate(
            flops=2 * rows * width * columns,
            bytes_accessed=2 * (width * columns + 2 * rows * columns),
            transcendentals=rows * columns,
        ),
    )(*tiles, weight)


def attention_kernel(
    info, proj, slope, normed, near, near_slope, near_normed, d_gated,
    gated, d_pre, near_d_pre, send, keep,
    factor, att_all, bent_all, attended, d_attended,
):
    width = normed.shape[1]
    halo = near.shape[0]
    block, core = info[0], info[1]
    ends = [info[2]]
    for user in range(1, 4):
        ends.append(ends[-1] + info[2 + user])
    columns = MOST * TILE
    lane = lax.broadcasted_iota(jnp.int32, (TILE, columns), 1)
    row = lax.broadcasted_iota(jnp.int32, (TILE, columns), 0)
    causal = lane - (columns - TILE) <= row
    for r in range(2):
        tile = 2 * block + r
        start, end = jnp.int32(0), ends[-1]
        for stop in ends:
            start = jnp.maximum(start, jnp.where(stop <= tile, stop, 0))
            end = jnp.minimum(end, jnp.where(stop > tile, stop, ends[-1]))
        live = (lane // TILE + (tile - (MOST - 1)) >= start) & causal
        events = jnp.full((TILE, columns), (end - start) * TILE, jnp.int32).astype(F32)
        factor[r] = jnp.where(live, 1.0 / events, 0.0)

    def head_slices(h):
        at = pl.multiple_of(h * HEAD, HEAD)
        return [pl.ds(part * width + at, HEAD) for part in range(4)]

    def forward(h, carry):
        _, at_v, at_q, at_k = head_slices(h)
        near_v, near_k = pl.ds(pl.multiple_of(h * HEAD, HEAD), HEAD), head_slices(h)[1]
        keys = jnp.concatenate([near[:, near_k], proj[:, at_k]], axis=0)
        values = jnp.concatenate([near[:, near_v], proj[:, at_v]], axis=0)
        for r in range(2):
            rows = slice(r * TILE, (r + 1) * TILE)
            window = slice(r * TILE, r * TILE + columns)
            scores = dot_nt(proj[rows, at_q], keys[window])
            silu, bent = silu_pair(scores * (0.5 * SCALE))
            att = (silu * factor[r]).astype(BF16)
            att_all[h, r] = att
            bent_all[h, r] = (bent * factor[r]).astype(BF16)
            attended[rows, near_v] = dot_nn(att, values[window])
        return carry

    lax.fori_loop(0, HEADS, forward, 0, unroll=2)

    for r in range(2):
        rows = slice(r * TILE, (r + 1) * TILE)
        gate = proj[rows, 0:width].astype(F32)
        normal, recip = normalize(attended[rows, :])
        gated[rows, :] = (normal * gate).astype(BF16)
        upstream = d_gated[rows, :]
        d_attended[rows, :] = norm_back(upstream * gate, normal, recip).astype(BF16)
        d_pre[rows, 0:width] = (upstream * normal * slope[rows, 0:width].astype(F32)).astype(BF16)

    def backward(h, carry):
        _, at_v, at_q, at_k = head_slices(h)
        near_v, near_k = pl.ds(pl.multiple_of(h * HEAD, HEAD), HEAD), head_slices(h)[1]
        keys = jnp.concatenate([near[:, near_k], proj[:, at_k]], axis=0)
        values = jnp.concatenate([near[:, near_v], proj[:, at_v]], axis=0)
        d_keys, d_values = [], []
        for r in range(2):
            rows = slice(r * TILE, (r + 1) * TILE)
            window = slice(r * TILE, r * TILE + columns)
            upstream = d_attended[rows, near_v]
            d_att = dot_nt(upstream, values[window])
            d_scores = (d_att * bent_all[h, r].astype(F32)).astype(BF16)
            d_query = dot_nn(d_scores, keys[window]) * SCALE
            d_pre[rows, at_q] = (d_query * slope[rows, at_q].astype(F32)).astype(BF16)
            d_keys.append(dot_tn(d_scores, proj[rows, at_q]))
            d_values.append(dot_tn(att_all[h, r], upstream))
        for (first, second), own_at, near_at, scaled in (
            (d_keys, at_k, near_k, SCALE),
            (d_values, at_v, near_v, 1.0),
        ):
            both = first[TILE:] + second[:-TILE]
            total = jnp.concatenate([first[:TILE], both, second[-TILE:]], axis=0) * scaled
            near_d_pre[:, near_at] = (
                total[:halo] * near_slope[:, near_at].astype(F32)
            ).astype(BF16)
            d_pre[:, own_at] = (total[halo:] * slope[:, own_at].astype(F32)).astype(BF16)
        return carry

    lax.fori_loop(0, HEADS, backward, 0, unroll=2)

    half = width // 2
    for out, side in ((send, 1 - core), (keep, core)):
        at = pl.multiple_of(side * half, half)
        d_key = jnp.concatenate(
            [near_d_pre[:, pl.ds(width + at, half)], d_pre[:, pl.ds(3 * width + at, half)]], axis=0
        )
        for n in range(0, width, 256):
            part = jnp.concatenate([near_normed[:, n : n + 256], normed[:, n : n + 256]], axis=0)
            out[n : n + 256, :] = dot_tn(part, d_key).astype(BF16)


def attention(info, proj, slope, normed, near, near_slope, near_normed, d_gated):
    rows, width = normed.shape
    halo = near.shape[0]
    shapes = [
        ((rows, width), BF16),
        ((rows, 4 * width), BF16),
        ((halo, 2 * width), BF16),
        ((width, width // 2), BF16),
        ((width, width // 2), BF16),
    ]
    return pl.pallas_call(
        attention_kernel,
        in_specs=[pl.BlockSpec(memory_space=pltpu.SMEM)] + [whole()] * 7,
        out_specs=[whole()] * 5,
        out_shape=[jax.ShapeDtypeStruct(*s) for s in shapes],
        scratch_shapes=[
            pltpu.VMEM((2, TILE, MOST * TILE), F32),
            pltpu.VMEM((HEADS, 2, TILE, MOST * TILE), BF16),
            pltpu.VMEM((HEADS, 2, TILE, MOST * TILE), BF16),
            pltpu.VMEM((rows, width), F32),
            pltpu.VMEM((rows, width), BF16),
        ],
        compiler_params=pltpu.CompilerParams(vmem_limit_bytes=40 * MIB),
        cost_estimate=pl.CostEstimate(
            flops=2 * 1500 * MIB, bytes_accessed=16 * MIB, transcendentals=MIB
        ),
    )(info, proj, slope, normed, near, near_slope, near_normed, d_gated)


def through_kernel(d_pre, near_d_pre, weight, own, other, far, odd, even, total, near_total):
    i = pl.program_id(0)

    @pl.when(i == 0)
    def _():
        total[...] = jnp.zeros_like(total)
        near_total[...] = jnp.zeros_like(near_total)

    total[...] += dot_nt(d_pre[...], weight[...])

    @pl.when((i // 2) % 2 == 1)
    def _():
        near_total[...] += dot_nt(near_d_pre[...], weight[...])

    @pl.when(i == pl.num_programs(0) - 1)
    def _():
        own[...] = total[:TILE, :]
        other[...] = total[TILE:, :].astype(BF16)
        far[...] = near_total[:TILE, :].astype(BF16)
        even[...] = near_total[TILE : 2 * TILE, :].astype(BF16)
        odd[...] = near_total[2 * TILE :, :].astype(BF16)


def through(d_pre, near_d_pre, weight):
    rows, halo, width = d_pre.shape[0], near_d_pre.shape[0], weight.shape[0]
    step = width // 2
    shape = (TILE, width)
    return pl.pallas_call(
        through_kernel,
        grid=(8,),
        in_specs=[
            pl.BlockSpec((rows, step), lambda i: (0, i)),
            pl.BlockSpec((halo, step), lambda i: (0, 2 * (i // 4) + jnp.where((i // 2) % 2 == 1, i % 2, 0))),
            pl.BlockSpec((width, step), lambda i: (0, i)),
        ],
        out_specs=[pl.BlockSpec(shape, lambda i: (0, 0))] * 5,
        out_shape=[jax.ShapeDtypeStruct(shape, F32)] + [jax.ShapeDtypeStruct(shape, BF16)] * 4,
        scratch_shapes=[pltpu.VMEM((rows, width), F32), pltpu.VMEM((halo, width), F32)],
        compiler_params=pltpu.CompilerParams(vmem_limit_bytes=32 * MIB),
        cost_estimate=pl.CostEstimate(
            flops=2 * width * width * (4 * rows + 2 * halo),
            bytes_accessed=8 * width * width + 8 * rows * width,
            transcendentals=0,
        ),
    )(d_pre, near_d_pre, weight)


def finish_kernel(info, events, back, own, even, other, odd, far, out):
    core = info[1]
    own_rows = pl.ds(pl.multiple_of(core * TILE, TILE), TILE)
    other_rows = pl.ds(pl.multiple_of((1 - core) * TILE, TILE), TILE)
    sums = (
        (own_rows, own[...] + even[...].astype(F32)),
        (other_rows, other[...].astype(F32) + odd[...].astype(F32) + far[...].astype(F32)),
    )
    for rows, d_normed in sums:
        normed_f, recip = normalize(events[rows, :].astype(F32))
        out[rows, :] = (back[rows, :].astype(F32) + norm_back(d_normed, normed_f, recip)).astype(BF16)


def finish(info, *arrays):
    return pl.pallas_call(
        finish_kernel,
        in_specs=[pl.BlockSpec(memory_space=pltpu.SMEM)] + [whole()] * 7,
        out_specs=whole(),
        out_shape=jax.ShapeDtypeStruct(arrays[0].shape, BF16),
        compiler_params=pltpu.CompilerParams(vmem_limit_bytes=24 * MIB),
        cost_estimate=pl.CostEstimate(flops=4 * MIB, bytes_accessed=4 * MIB, transcendentals=0),
    )(info, *arrays)


def shards(events, lengths, weight_in, weight_out, cotangent):
    pairs = lax.axis_size(SEQ)
    chips = pairs // 2
    pair = lax.axis_index(SEQ)
    core = lax.axis_index("core")
    block = jnp.where(core == 0, pair // 2, pairs - 1 - pair // 2)
    info = jnp.concatenate([jnp.stack([block, core]).astype(jnp.int32), lengths[0]])
    near_odd, near_even, onward, far_odd = routes(pairs)
    swap = [(i, i ^ 1) for i in range(pairs)]

    local = events.reshape(2 * TILE, -1)
    back = cotangent.reshape(2 * TILE, -1)
    width = local.shape[1]

    def split(array):
        mine = lax.dynamic_slice_in_dim(array, core * TILE, TILE, 0)
        other = lax.dynamic_slice_in_dim(array, (1 - core) * TILE, TILE, 0)
        return mine, other

    mine, other = split(local)
    tile_1 = move(other, near_odd)
    tile_2 = move(mine, near_even)
    second = move(other, swap)
    tile_3 = move(tile_1, onward)
    back_mine, back_other = split(back)
    back_second = move(back_other, swap)

    normed, proj, slope = project([mine, second], weight_in, 4 * width, lambda i: i)
    d_gated = dot_nt(jnp.concatenate([back_mine, back_second], axis=0), weight_out)
    near_normed, near, near_slope = project(
        [tile_3, tile_2, tile_1], weight_in, 2 * width, lambda i: 2 + i + 4 * (i // 2) - 2 * (i // 2)
    )
    gated, d_pre, near_d_pre, send, keep = attention(
        info, proj, slope, normed, near, near_slope, near_normed, d_gated
    )

    total = keep.astype(F32) + move(send, swap).astype(F32)
    pieces = lax.all_to_all(
        total.astype(BF16), ("dp", "y", "x"), split_axis=0, concat_axis=0, tiled=True
    )
    count = lax.axis_size(("dp", "y", "x"))
    share = jnp.sum(pieces.reshape(count, width // count, width // 2).astype(F32), axis=0)
    rows = width // count // 2
    kept = lax.dynamic_slice_in_dim(share, core * rows, rows, 0)
    given = lax.dynamic_slice_in_dim(share, (1 - core) * rows, rows, 0)
    taken = move(given, swap)
    summed = jnp.where(
        core == 0,
        jnp.concatenate([kept, taken], axis=1),
        jnp.concatenate([taken, kept], axis=1),
    )

    own_d, other_d, far_d, odd_d, even_d = through(d_pre, near_d_pre, weight_in)
    other_in = move(other_d, swap)
    odd_in = move(odd_d, reverse(near_odd))
    even_in = move(even_d, reverse(near_even))
    far_in = move(far_d, reverse(far_odd))
    event_grads = finish(info, local, back, own_d, even_in, other_in, odd_in, far_in)

    contexts = jnp.concatenate([mine, second], axis=0).astype(F32)
    outs = (contexts + dot_nn(gated, weight_out)).astype(BF16)
    out_mine, out_second = outs[:TILE], outs[TILE:]
    out_other = move(out_second, swap)
    layer_out = jnp.where(
        core == 0,
        jnp.concatenate([out_mine, out_other], axis=0),
        jnp.concatenate([out_other, out_mine], axis=0),
    )
    return (layer_out.reshape(events.shape), event_grads.reshape(events.shape), summed)


def solution(mesh):
    devices = mesh.devices
    fine = Mesh(devices.reshape(devices.shape[0], 4, 4, 2), ("dp",) + SEQ)
    every = P("dp", SEQ, None, None)
    return jax.shard_map(
        shards,
        mesh=fine,
        in_specs=(every, P("dp", None), P(), P(), every),
        out_specs=(every, every, P(("dp",) + SEQ, None)),
        check_vma=False,
    )
```

```python
import jax
import jax.numpy as jnp
from jax import lax
from jax.experimental import pallas as pl
from jax.experimental.pallas import tpu as pltpu
from jax.sharding import Mesh, PartitionSpec as P

HEADS = 8
HEAD = 128
TILE = 128
MOST = 4
EPSILON = 1e-06
SCALE = HEAD ** (-0.5)
SEQ = ("y", "x", "core")
MIB = 1024 * 1024
SCOPED = 16 * MIB
TINY = pl.CostEstimate(flops=1024, bytes_accessed=1024, transcendentals=0)

F32 = jnp.float32
BF16 = jnp.bfloat16


def chain_device(block, chips):
    return 2 * block if block < chips else 2 * (2 * chips - 1 - block) + 1


def chain_block(core):
    pair = lax.axis_index(SEQ)
    return jnp.where(core == 0, pair // 2, lax.axis_size(SEQ) - 1 - pair // 2)


def tile_owner(tile, pairs):
    return tile if tile < pairs else 2 * pairs - 1 - tile


def routes(pairs):
    chips = pairs // 2
    place = [chain_device(block, chips) for block in range(pairs)]
    near_odd = [(tile_owner(2 * b - 1, pairs), place[b]) for b in range(1, pairs)]
    near_even = [(tile_owner(2 * b - 2, pairs), place[b]) for b in range(1, pairs)]
    onward = [(place[b - 1], place[b]) for b in range(2, pairs)]
    back = [(place[b], place[b - 1]) for b in range(1, pairs)]
    far_back = [(place[b], tile_owner(2 * b - 3, pairs)) for b in range(2, pairs)]
    return near_odd, near_even, onward, back, far_back


def move(block, route):
    return lax.ppermute(block, SEQ, route)


def normalize(values):
    centre = jnp.mean(values, axis=-1, keepdims=True)
    centred = values - centre
    spread = jnp.mean(centred * centred, axis=-1, keepdims=True)
    recip = lax.rsqrt(spread + EPSILON)
    return centred * recip, recip


def norm_back(upstream, normed_f, recip):
    first = jnp.mean(upstream, axis=-1, keepdims=True)
    second = jnp.mean(upstream * normed_f, axis=-1, keepdims=True)
    return recip * (upstream - first - normed_f * second)


def silu_pair(half):
    bend = jnp.tanh(half)
    silu = half + half * bend
    sigmoid = 0.5 + 0.5 * bend
    return silu, sigmoid + silu * (1.0 - sigmoid)


def dot_nn(left, right):
    return lax.dot_general(left, right, (((1,), (0,)), ((), ())), preferred_element_type=F32)


def dot_nt(left, right):
    return lax.dot_general(left, right, (((1,), (1,)), ((), ())), preferred_element_type=F32)


def dot_tn(left, right):
    return lax.dot_general(left, right, (((0,), (0,)), ((), ())), preferred_element_type=F32)


def whole():
    return pl.BlockSpec(memory_space=pltpu.VMEM)


def remote():
    return pl.BlockSpec(memory_space=pltpu.HBM)


def split_kernel(array, mine, other, sems):
    core = lax.axis_index("core")
    copies = [
        pltpu.make_async_copy(array.at[pl.ds(pl.multiple_of(at * TILE, TILE), TILE)], out, sems.at[n])
        for n, (at, out) in enumerate(((1 - core, other), (core, mine)))
    ]
    for copy in copies:
        copy.start()
    for copy in copies:
        copy.wait()


def split(array, cost):
    tile = jax.ShapeDtypeStruct((TILE, array.shape[1]), BF16)
    return pl.pallas_call(
        split_kernel,
        in_specs=[remote()],
        out_specs=[whole()] * 2,
        out_shape=[tile, tile],
        scratch_shapes=[pltpu.SemaphoreType.DMA((2,))],
        compiler_params=pltpu.CompilerParams(vmem_limit_bytes=2 * MIB),
        cost_estimate=pl.CostEstimate(flops=0, bytes_accessed=cost, transcendentals=0),
    )(array)


def project_columns(normed, weight, columns, proj, slope, copies):
    step = 512
    for n, at in enumerate(columns):
        copies[n].wait()
        silu, bent = silu_pair(0.5 * dot_nn(normed[...], weight[:, n * step : (n + 1) * step]))
        proj[:, n * step : (n + 1) * step] = silu.astype(BF16)
        slope[:, n * step : (n + 1) * step] = bent.astype(BF16)


def fetch_columns(weight, columns, held, sems):
    step = 512
    copies = [
        pltpu.make_async_copy(weight.at[:, at : at + step], held.at[:, n * step : (n + 1) * step], sems.at[n])
        for n, at in enumerate(columns)
    ]
    for copy in copies:
        copy.start()
    return copies


def project_kernel(
    mine, second, back_mine, back_second, weight, weight_out, normed, proj, slope, d_gated,
    held, held_out, sems,
):
    width = weight.shape[0]
    columns = range(0, 4 * width, 512)
    copies = fetch_columns(weight, columns, held, sems)
    last = pltpu.make_async_copy(weight_out, held_out, sems.at[len(copies)])
    last.start()
    for r, tile in enumerate((mine, second)):
        rows = slice(r * TILE, (r + 1) * TILE)
        normed[rows, :] = normalize(tile[...].astype(F32))[0].astype(BF16)
    project_columns(normed, held, columns, proj, slope, copies)
    last.wait()
    for n in range(0, width, 256):
        part = held_out[n : n + 256, :]
        d_gated[:TILE, n : n + 256] = dot_nt(back_mine[...], part)
        d_gated[TILE:, n : n + 256] = dot_nt(back_second[...], part)


def project(mine, second, back_mine, back_second, weight, weight_out):
    width, columns = weight.shape
    rows = 2 * TILE
    shapes = [((rows, width), BF16), ((rows, columns), BF16), ((rows, columns), BF16), ((rows, width), F32)]
    return pl.pallas_call(
        project_kernel,
        in_specs=[whole()] * 4 + [remote()] * 2,
        out_specs=[whole()] * 4,
        out_shape=[jax.ShapeDtypeStruct(*s) for s in shapes],
        scratch_shapes=[
            pltpu.VMEM(weight.shape, BF16),
            pltpu.VMEM(weight_out.shape, BF16),
            pltpu.SemaphoreType.DMA((columns // 512 + 1,)),
        ],
        compiler_params=pltpu.CompilerParams(vmem_limit_bytes=47 * MIB),
        cost_estimate=pl.CostEstimate(
            flops=2 * rows * width * (columns + width),
            bytes_accessed=2 * (width * columns + 2 * rows * columns),
            transcendentals=rows * columns,
        ),
    )(mine, second, back_mine, back_second, weight, weight_out)


def project_near_kernel(far, even, odd, weight, normed, proj, slope, held, sems):
    width = weight.shape[0]
    columns = [part * width + at for part in (1, 3) for at in range(0, width, 512)]
    copies = fetch_columns(weight, columns, held, sems)
    for r, tile in enumerate((far, even, odd)):
        rows = slice(r * TILE, (r + 1) * TILE)
        normed[rows, :] = normalize(tile[...].astype(F32))[0].astype(BF16)
    project_columns(normed, held, columns, proj, slope, copies)


def project_near(tiles, weight):
    rows, width = 3 * TILE, weight.shape[0]
    shapes = [((rows, width), BF16), ((rows, 2 * width), BF16), ((rows, 2 * width), BF16)]
    return pl.pallas_call(
        project_near_kernel,
        in_specs=[whole()] * 3 + [remote()],
        out_specs=[whole()] * 3,
        out_shape=[jax.ShapeDtypeStruct(*s) for s in shapes],
        scratch_shapes=[pltpu.VMEM((width, 2 * width), BF16), pltpu.SemaphoreType.DMA((4,))],
        compiler_params=pltpu.CompilerParams(vmem_limit_bytes=44 * MIB),
        cost_estimate=pl.CostEstimate(
            flops=4 * rows * width * width, bytes_accessed=8 * width * width, transcendentals=2 * rows * width
        ),
    )(*tiles, weight)


def attention_kernel(
    lengths, proj, slope, near, near_slope, d_gated,
    gated, d_pre, near_d_pre,
    factor, att_all, bent_all, attended, d_attended,
):
    width = gated.shape[1]
    halo = near.shape[0]
    core = lax.axis_index("core")
    block = chain_block(core)
    ends = [lengths[0, 0]]
    for user in range(1, lengths.shape[1]):
        ends.append(ends[-1] + lengths[0, user])
    columns = MOST * TILE
    lane = lax.broadcasted_iota(jnp.int32, (TILE, columns), 1)
    row = lax.broadcasted_iota(jnp.int32, (TILE, columns), 0)
    causal = lane - (columns - TILE) <= row
    for r in range(2):
        tile = 2 * block + r
        start, end = jnp.int32(0), ends[-1]
        for stop in ends:
            start = jnp.maximum(start, jnp.where(stop <= tile, stop, 0))
            end = jnp.minimum(end, jnp.where(stop > tile, stop, ends[-1]))
        live = (lane // TILE + (tile - (MOST - 1)) >= start) & causal
        events = jnp.full((TILE, columns), (end - start) * TILE, jnp.int32).astype(F32)
        factor[r] = jnp.where(live, 1.0 / events, 0.0)

    def head_slices(h):
        at = pl.multiple_of(h * HEAD, HEAD)
        return [pl.ds(part * width + at, HEAD) for part in range(4)]

    def forward(h, carry):
        _, at_v, at_q, at_k = head_slices(h)
        near_v, near_k = pl.ds(pl.multiple_of(h * HEAD, HEAD), HEAD), head_slices(h)[1]
        keys = jnp.concatenate([near[:, near_k], proj[:, at_k]], axis=0)
        values = jnp.concatenate([near[:, near_v], proj[:, at_v]], axis=0)
        for r in range(2):
            rows = slice(r * TILE, (r + 1) * TILE)
            window = slice(r * TILE, r * TILE + columns)
            scores = dot_nt(proj[rows, at_q], keys[window])
            silu, bent = silu_pair(scores * (0.5 * SCALE))
            att = (silu * factor[r]).astype(BF16)
            att_all[h, r] = att
            bent_all[h, r] = (bent * factor[r]).astype(BF16)
            attended[rows, near_v] = dot_nn(att, values[window])
        return carry

    lax.fori_loop(0, HEADS, forward, 0, unroll=2)

    for r in range(2):
        rows = slice(r * TILE, (r + 1) * TILE)
        gate = proj[rows, 0:width].astype(F32)
        normal, recip = normalize(attended[rows, :])
        gated[rows, :] = (normal * gate).astype(BF16)
        upstream = d_gated[rows, :]
        d_attended[rows, :] = norm_back(upstream * gate, normal, recip).astype(BF16)
        d_pre[rows, 0:width] = (upstream * normal * slope[rows, 0:width].astype(F32)).astype(BF16)

    def backward(h, carry):
        _, at_v, at_q, at_k = head_slices(h)
        near_v, near_k = pl.ds(pl.multiple_of(h * HEAD, HEAD), HEAD), head_slices(h)[1]
        keys = jnp.concatenate([near[:, near_k], proj[:, at_k]], axis=0)
        values = jnp.concatenate([near[:, near_v], proj[:, at_v]], axis=0)
        d_keys, d_values = [], []
        for r in range(2):
            rows = slice(r * TILE, (r + 1) * TILE)
            window = slice(r * TILE, r * TILE + columns)
            upstream = d_attended[rows, near_v]
            d_att = dot_nt(upstream, values[window])
            d_scores = (d_att * bent_all[h, r].astype(F32)).astype(BF16)
            d_query = dot_nn(d_scores, keys[window]) * SCALE
            d_pre[rows, at_q] = (d_query * slope[rows, at_q].astype(F32)).astype(BF16)
            d_keys.append(dot_tn(d_scores, proj[rows, at_q]))
            d_values.append(dot_tn(att_all[h, r], upstream))
        for (first, second), own_at, near_at, scaled in (
            (d_keys, at_k, near_k, SCALE),
            (d_values, at_v, near_v, 1.0),
        ):
            both = first[TILE:] + second[:-TILE]
            total = jnp.concatenate([first[:TILE], both, second[-TILE:]], axis=0) * scaled
            near_d_pre[:, near_at] = (
                total[:halo] * near_slope[:, near_at].astype(F32)
            ).astype(BF16)
            d_pre[:, own_at] = (total[halo:] * slope[:, own_at].astype(F32)).astype(BF16)
        return carry

    lax.fori_loop(0, HEADS, backward, 0, unroll=2)


def attention(lengths, proj, slope, near, near_slope, d_gated):
    rows, width = d_gated.shape
    halo = near.shape[0]
    shapes = [((rows, width), BF16), ((rows, 4 * width), BF16), ((halo, 2 * width), BF16)]
    return pl.pallas_call(
        attention_kernel,
        in_specs=[pl.BlockSpec(memory_space=pltpu.SMEM)] + [whole()] * 5,
        out_specs=[whole()] * 3,
        out_shape=[jax.ShapeDtypeStruct(*s) for s in shapes],
        scratch_shapes=[
            pltpu.VMEM((2, TILE, MOST * TILE), F32),
            pltpu.VMEM((HEADS, 2, TILE, MOST * TILE), BF16),
            pltpu.VMEM((HEADS, 2, TILE, MOST * TILE), BF16),
            pltpu.VMEM((rows, width), F32),
            pltpu.VMEM((rows, width), BF16),
        ],
        compiler_params=pltpu.CompilerParams(vmem_limit_bytes=SCOPED),
        cost_estimate=pl.CostEstimate(
            flops=2 * 800 * MIB, bytes_accessed=16 * MIB, transcendentals=MIB
        ),
    )(lengths, proj, slope, near, near_slope, d_gated)


def key_grad_kernel(near_normed, normed, near_d_pre, d_pre, send, keep):
    width = normed.shape[1]
    even = lax.axis_index("core") == 0
    half = width // 2
    side, depth = keep.shape[:2]
    d_key = jnp.concatenate([near_d_pre[:, width:], d_pre[:, 3 * width :]], axis=0)
    upper = lax.broadcasted_iota(jnp.int32, (1, 8, half), 1) < 4
    step = width // depth
    for z in range(depth):
        at = slice(z * step, (z + 1) * step)
        part = jnp.concatenate([near_normed[:, at], normed[:, at]], axis=0)
        grad = dot_tn(part, d_key).reshape(side * side, 8, width)
        left, right = grad[:, :, :half], grad[:, :, half:]
        first = jnp.where(upper, left, pltpu.roll(right, 4, 1))
        last = jnp.where(upper, pltpu.roll(left, 4, 1), right)
        kept = jnp.where(even, first, last).astype(BF16)
        sent = jnp.where(even, last, first).astype(BF16)
        for y in range(side):
            for x in range(side):
                by_row, by_column = y * side + x, x * side + y
                keep[y, z, x] = jnp.where(even, kept[by_column], kept[by_row])
                send[y, z, x] = jnp.where(even, sent[by_row], sent[by_column])


def key_grad(near_normed, normed, near_d_pre, d_pre):
    width = normed.shape[1]
    depth, side = lax.axis_size("dp"), lax.axis_size("x")
    shape = jax.ShapeDtypeStruct((side, depth, side, 8, width // 2), BF16)
    return pl.pallas_call(
        key_grad_kernel,
        in_specs=[whole()] * 4,
        out_specs=[whole()] * 2,
        out_shape=[shape, shape],
        compiler_params=pltpu.CompilerParams(vmem_limit_bytes=SCOPED),
        cost_estimate=TINY,
    )(near_normed, normed, near_d_pre, d_pre)


def ring_place():
    return jnp.where(lax.axis_index("core") == 0, lax.axis_index("x"), lax.axis_index("y"))


def ring_route(shift):
    route = []
    for pair in range(32):
        y, x, core = pair // 8, pair // 2 % 4, pair % 2
        y, x = (y, (x + shift) % 4) if core == 0 else ((y + shift) % 4, x)
        route.append((pair, y * 8 + x * 2 + core))
    return route


def ring_first_kernel(keep, received, total, up, down):
    place = ring_place()
    half = up.shape[0]
    total[...] = (keep[...].astype(F32) + received[...].astype(F32)).astype(BF16)
    opposite = total.at[lax.rem(place + 2, 4)]
    up[...] = opposite[:half]
    down[...] = opposite[half:]


def ring_second_kernel(total, from_below, from_above, up, down):
    place = ring_place()
    half = from_below.shape[0]
    above, below = total.at[lax.rem(place + 1, 4)], total.at[lax.rem(place + 3, 4)]
    up[:half] = (above[:half].astype(F32) + from_below[...].astype(F32)).astype(BF16)
    up[half:] = above[half:]
    down[:half] = below[:half]
    down[half:] = (below[half:].astype(F32) + from_above[...].astype(F32)).astype(BF16)


def ring_third_kernel(total, from_below, from_above, column):
    own = total.at[ring_place()]
    column[...] = (
        own[...].astype(F32) + from_below[...].astype(F32) + from_above[...].astype(F32)
    ).astype(BF16)


def on_device(kernel, shapes, *arrays):
    return pl.pallas_call(
        kernel,
        in_specs=[whole()] * len(arrays),
        out_specs=[whole()] * len(shapes),
        out_shape=[jax.ShapeDtypeStruct(shape, BF16) for shape in shapes],
        compiler_params=pltpu.CompilerParams(vmem_limit_bytes=SCOPED),
        cost_estimate=TINY,
    )(*arrays)


def near_through_kernel(near_d_pre, weight, far, out):
    width = weight.shape[0]
    step = 256
    for n in range(0, width, step):
        at = slice(n, n + step)
        near = dot_nt(near_d_pre[:, :width], weight[at, width : 2 * width])
        near = (near + dot_nt(near_d_pre[:, width:], weight[at, 3 * width :])).astype(BF16)
        far[:, at] = near[:TILE]
        out[:, at] = near[TILE:]


def near_through(near_d_pre, weight):
    halo, width = near_d_pre.shape[0], weight.shape[0]
    return pl.pallas_call(
        near_through_kernel,
        in_specs=[whole()] * 2,
        out_specs=[whole()] * 2,
        out_shape=[
            jax.ShapeDtypeStruct((TILE, width), BF16), jax.ShapeDtypeStruct((halo - TILE, width), BF16)
        ],
        compiler_params=pltpu.CompilerParams(vmem_limit_bytes=SCOPED),
        cost_estimate=TINY,
    )(near_d_pre, weight)


def through_kernel(d_pre, gated, mine, second, weight, weight_out, d_normed, outs):
    width = weight.shape[0]
    step = 256
    for n in range(0, width, step):
        at = slice(n, n + step)
        d_normed[:, at] = dot_nt(d_pre[...], weight[at, :])
        update = dot_nn(gated[...], weight_out[:, at])
        outs[:TILE, at] = (mine[:, at].astype(F32) + update[:TILE]).astype(BF16)
        outs[TILE:, at] = (second[:, at].astype(F32) + update[TILE:]).astype(BF16)


def through(d_pre, gated, mine, second, weight, weight_out):
    rows, width = d_pre.shape[0], weight.shape[0]
    return pl.pallas_call(
        through_kernel,
        in_specs=[whole()] * 6,
        out_specs=[whole()] * 2,
        out_shape=[
            jax.ShapeDtypeStruct((rows, width), F32), jax.ShapeDtypeStruct((rows, width), BF16)
        ],
        compiler_params=pltpu.CompilerParams(vmem_limit_bytes=SCOPED),
        cost_estimate=TINY,
    )(d_pre, gated, mine, second, weight, weight_out)


def merge_kernel(d_normed, arrived, outs, own, given):
    own[...] = d_normed[:TILE, :] + arrived[:TILE, :].astype(F32)
    given[:TILE, :] = outs[TILE:, :]
    given[TILE:, :] = (d_normed[TILE:, :] + arrived[TILE:, :].astype(F32)).astype(BF16)


def merge(d_normed, arrived, outs):
    rows, width = outs.shape
    return pl.pallas_call(
        merge_kernel,
        in_specs=[whole()] * 3,
        out_specs=[whole()] * 2,
        out_shape=[
            jax.ShapeDtypeStruct((TILE, width), F32),
            jax.ShapeDtypeStruct((rows, width), BF16),
        ],
        compiler_params=pltpu.CompilerParams(vmem_limit_bytes=SCOPED),
        cost_estimate=TINY,
    )(d_normed, arrived, outs)


def finish_kernel(
    events, back, outs, own, taken, far, layer_out, event_grads, layer, grads, sems
):
    core = lax.axis_index("core")
    kept = pl.ds(pl.multiple_of(core * TILE, TILE), TILE)
    swapped = pl.ds(pl.multiple_of((1 - core) * TILE, TILE), TILE)
    layer[0] = outs[:TILE, :]
    layer[1] = taken[:TILE, :]
    stores = [
        pltpu.make_async_copy(layer.at[r], layer_out.at[rows], sems.at[r])
        for r, rows in enumerate((kept, swapped))
    ]
    for copy in stores:
        copy.start()
    sums = (
        (kept, own[...]),
        (swapped, taken[TILE:, :].astype(F32) + far[...].astype(F32)),
    )
    for r, (rows, d_normed) in enumerate(sums):
        normed_f, recip = normalize(events[rows, :].astype(F32))
        grads[r] = (back[rows, :].astype(F32) + norm_back(d_normed, normed_f, recip)).astype(BF16)
        stores.append(pltpu.make_async_copy(grads.at[r], event_grads.at[rows], sems.at[2 + r]))
        stores[-1].start()
    for copy in stores:
        copy.wait()


def finish(events, back, outs, own, taken, far):
    rows, width = events.shape
    return pl.pallas_call(
        finish_kernel,
        in_specs=[whole()] * 6,
        out_specs=[remote()] * 2,
        out_shape=[jax.ShapeDtypeStruct((rows, width), BF16)] * 2,
        scratch_shapes=[
            pltpu.VMEM((2, TILE, width), BF16),
            pltpu.VMEM((2, TILE, width), BF16),
            pltpu.SemaphoreType.DMA((4,)),
        ],
        compiler_params=pltpu.CompilerParams(vmem_limit_bytes=SCOPED),
        cost_estimate=pl.CostEstimate(flops=4 * MIB, bytes_accessed=4 * MIB, transcendentals=0),
    )(events, back, outs, own, taken, far)


def sum_kernel(parts, out):
    total = parts[0].astype(F32)
    for n in range(1, parts.shape[0]):
        total = total + parts[n].astype(F32)
    out[:, : total.shape[1]] = total[:4]
    out[:, total.shape[1] :] = total[4:]


def sum_parts(parts):
    return pl.pallas_call(
        sum_kernel,
        in_specs=[whole()],
        out_specs=whole(),
        out_shape=jax.ShapeDtypeStruct((4, 2 * parts.shape[-1]), F32),
        compiler_params=pltpu.CompilerParams(vmem_limit_bytes=SCOPED),
        cost_estimate=TINY,
    )(parts)


def last_groups():
    place = lambda z, y, x, core: ((z * 4 + y) * 4 + x) * 2 + core
    even = [[place(z, y, x, 0) for z in range(8) for y in range(4)] for x in range(4)]
    odd = [[place(z, y, x, 1) for z in range(8) for x in range(4)] for y in range(4)]
    return even + odd


def shards(events, lengths, weight_in, weight_out, cotangent):
    pairs = lax.axis_size(SEQ)
    near_odd, near_even, onward, backward, far_back = routes(pairs)
    swap = [(i, i ^ 1) for i in range(pairs)]
    local = events.reshape(2 * TILE, -1)
    back = cotangent.reshape(2 * TILE, -1)

    mine, other = split(local, 24 * MIB)
    odd = move(other, near_odd)
    even = move(mine, near_even)
    second = move(other, swap)
    far = move(odd, onward)
    back_mine, back_other = split(back, MIB)
    back_second = move(back_other, swap)

    normed, proj, slope, d_gated = project(mine, second, back_mine, back_second, weight_in, weight_out)
    far, even, odd, proj = lax.optimization_barrier((far, even, odd, proj))
    near_normed, near, near_slope = project_near([far, even, odd], weight_in)
    gated, d_pre, near_d_pre = attention(lengths, proj, slope, near, near_slope, d_gated)

    tie = lax.optimization_barrier
    send, keep = key_grad(near_normed, normed, near_d_pre, d_pre)
    received = move(send, swap)
    near_d_pre, send = tie((near_d_pre, send))
    far_d, near_d = near_through(near_d_pre, weight_in)
    arrived = move(near_d, backward)
    received, near_d = tie((received, near_d))

    block = keep.shape[1:]
    half = (block[0] // 2,) + block[1:]
    total, up, down = on_device(ring_first_kernel, [keep.shape, half, half], keep, received)
    from_below, from_above = move(up, ring_route(1)), move(down, ring_route(-1))
    d_pre, total = tie((d_pre, total))
    d_normed, outs = through(d_pre, gated, mine, second, weight_in, weight_out)
    from_below, from_above, d_normed = tie((from_below, from_above, d_normed))
    up, down = on_device(ring_second_kernel, [block, block], total, from_below, from_above)
    from_below, from_above = move(up, ring_route(1)), move(down, ring_route(-1))
    own, given = merge(d_normed, arrived, outs)
    far_in = move(far_d, far_back)
    from_below, from_above, own, far_in = tie((from_below, from_above, own, far_in))
    (column,) = on_device(ring_third_kernel, [block], total, from_below, from_above)
    column = column.reshape((block[0] * block[1],) + block[2:])
    parts = lax.all_to_all(
        column, ("dp",) + SEQ, split_axis=0, concat_axis=0, tiled=True, axis_index_groups=last_groups()
    )
    taken = move(given, swap)
    layer_out, event_grads = finish(local, back, outs, own, taken, far_in)
    summed = sum_parts(parts)
    return (layer_out.reshape(events.shape), event_grads.reshape(events.shape), summed)


def solution(mesh):
    devices = mesh.devices
    fine = Mesh(devices.reshape(devices.shape[0], 4, 4, 2), ("dp",) + SEQ)
    every = P("dp", SEQ, None, None)
    return jax.shard_map(
        shards,
        mesh=fine,
        in_specs=(every, P("dp", None), P(), P(), every),
        out_specs=(every, every, P(("dp",) + SEQ, None)),
        check_vma=False,
    )
```

```python
import jax
import jax.numpy as jnp
from jax import lax
from jax.experimental import pallas as pl
from jax.experimental.pallas import tpu as pltpu
from jax.sharding import Mesh, PartitionSpec as P

HEADS = 8
HEAD = 128
TILE = 128
MOST = 4
EPSILON = 1e-06
SCALE = HEAD ** (-0.5)
SEQ = ("y", "x", "core")
MIB = 1024 * 1024
SCOPED = 16 * MIB
TINY = pl.CostEstimate(flops=1024, bytes_accessed=1024, transcendentals=0)

F32 = jnp.float32
BF16 = jnp.bfloat16


def chain_device(block, chips):
    return 2 * block if block < chips else 2 * (2 * chips - 1 - block) + 1


def chain_block(core):
    pair = lax.axis_index(SEQ)
    return jnp.where(core == 0, pair // 2, lax.axis_size(SEQ) - 1 - pair // 2)


def tile_owner(tile, pairs):
    return tile if tile < pairs else 2 * pairs - 1 - tile


def routes(pairs):
    chips = pairs // 2
    place = [chain_device(block, chips) for block in range(pairs)]
    onward = [(place[b - 1], place[b]) for b in range(1, pairs)]
    far = [(tile_owner(2 * b - 3, pairs), place[b]) for b in range(2, pairs)]
    back = [(place[b], place[b - 1]) for b in range(1, pairs)]
    far_back = [(place[b], tile_owner(2 * b - 3, pairs)) for b in range(2, pairs)]
    return onward, far, back, far_back


def move(block, route):
    return lax.ppermute(block, SEQ, route)


def normalize(values):
    centre = jnp.mean(values, axis=-1, keepdims=True)
    centred = values - centre
    spread = jnp.mean(centred * centred, axis=-1, keepdims=True)
    recip = lax.rsqrt(spread + EPSILON)
    return centred * recip, recip


def norm_back(upstream, normed_f, recip):
    first = jnp.mean(upstream, axis=-1, keepdims=True)
    second = jnp.mean(upstream * normed_f, axis=-1, keepdims=True)
    return recip * (upstream - first - normed_f * second)


def silu_pair(half):
    rise = 1.0 + jnp.tanh(half)
    silu = half * rise
    return silu, rise * ((0.5 + half) - 0.5 * silu)


def dot_nn(left, right):
    return lax.dot_general(left, right, (((1,), (0,)), ((), ())), preferred_element_type=F32)


def dot_nt(left, right):
    return lax.dot_general(left, right, (((1,), (1,)), ((), ())), preferred_element_type=F32)


def dot_tn(left, right):
    return lax.dot_general(left, right, (((0,), (0,)), ((), ())), preferred_element_type=F32)


def whole():
    return pl.BlockSpec(memory_space=pltpu.VMEM)


def remote():
    return pl.BlockSpec(memory_space=pltpu.HBM)


def split_kernel(array, mine, other, sems):
    core = lax.axis_index("core")
    copies = [
        pltpu.make_async_copy(array.at[pl.ds(pl.multiple_of(at * TILE, TILE), TILE)], out, sems.at[n])
        for n, (at, out) in enumerate(((1 - core, other), (core, mine)))
    ]
    for copy in copies:
        copy.start()
    for copy in copies:
        copy.wait()


def split(array):
    tile = jax.ShapeDtypeStruct((TILE, array.shape[1]), BF16)
    return pl.pallas_call(
        split_kernel,
        in_specs=[remote()],
        out_specs=[whole()] * 2,
        out_shape=[tile, tile],
        scratch_shapes=[pltpu.SemaphoreType.DMA((2,))],
        compiler_params=pltpu.CompilerParams(vmem_limit_bytes=2 * MIB),
        cost_estimate=pl.CostEstimate(flops=8 * 1024 * MIB, bytes_accessed=24 * MIB, transcendentals=0),
    )(array)


def project_columns(normed, weight, columns, proj, slope):
    step = 512
    for n, at in enumerate(columns):
        pre = dot_nn(normed[...], weight[:, at : at + step])
        silu, bent = silu_pair(0.5 * pre)
        proj[:, n * step : (n + 1) * step] = silu.astype(BF16)
        slope[:, n * step : (n + 1) * step] = bent.astype(BF16)


def normalize_kernel(mine, second, normed):
    for r, tile in enumerate((mine, second)):
        rows = slice(r * TILE, (r + 1) * TILE)
        normed[rows, :] = normalize(tile[...].astype(F32))[0].astype(BF16)


def normalize_block(mine, second):
    rows, width = mine.shape
    return pl.pallas_call(
        normalize_kernel,
        in_specs=[whole()] * 2,
        out_specs=whole(),
        out_shape=jax.ShapeDtypeStruct((2 * rows, width), BF16),
        compiler_params=pltpu.CompilerParams(vmem_limit_bytes=2 * MIB),
        cost_estimate=pl.CostEstimate(flops=1024 * MIB, bytes_accessed=MIB, transcendentals=0),
    )(mine, second)


def project_kernel(normed, back_mine, back_second, weight_in, weight_out, proj, slope, d_gated):
    width = weight_in.shape[0]
    project_columns(normed, weight_in, range(0, 4 * width, 512), proj, slope)
    for n in range(0, width, 256):
        part = weight_out[n : n + 256, :]
        d_gated[:TILE, n : n + 256] = dot_nt(back_mine[...], part)
        d_gated[TILE:, n : n + 256] = dot_nt(back_second[...], part)


def project(normed, back_mine, back_second, weight, weight_out):
    width, columns = weight.shape
    rows = 2 * TILE
    shapes = [((rows, columns), BF16), ((rows, columns), BF16), ((rows, width), F32)]
    return pl.pallas_call(
        project_kernel,
        in_specs=[whole()] * 5,
        out_specs=[whole()] * 3,
        out_shape=[jax.ShapeDtypeStruct(*s) for s in shapes],
        compiler_params=pltpu.CompilerParams(vmem_limit_bytes=SCOPED),
        cost_estimate=pl.CostEstimate(
            flops=2 * rows * width * (columns + width),
            bytes_accessed=2 * (width * columns + 2 * rows * columns),
            transcendentals=rows * columns,
        ),
    )(normed, back_mine, back_second, weight, weight_out)


def project_near_kernel(far, near, weight, normed, proj, slope):
    width = weight.shape[0]
    normed[:TILE, :] = normalize(far[...].astype(F32))[0].astype(BF16)
    normed[TILE:, :] = near[...]
    columns = [part * width + at for part in (1, 3) for at in range(0, width, 512)]
    project_columns(normed, weight, columns, proj, slope)


def project_near(far, near, weight):
    rows, width = 3 * TILE, weight.shape[0]
    shapes = [((rows, width), BF16), ((rows, 2 * width), BF16), ((rows, 2 * width), BF16)]
    return pl.pallas_call(
        project_near_kernel,
        in_specs=[whole()] * 3,
        out_specs=[whole()] * 3,
        out_shape=[jax.ShapeDtypeStruct(*s) for s in shapes],
        compiler_params=pltpu.CompilerParams(vmem_limit_bytes=SCOPED),
        cost_estimate=pl.CostEstimate(
            flops=4 * rows * width * width, bytes_accessed=8 * width * width, transcendentals=2 * rows * width
        ),
    )(far, near, weight)


def attention_kernel(
    lengths, proj, slope, near, near_slope, d_gated,
    gated, d_pre, near_d_pre,
    factor, att_all, bent_all, attended, d_attended,
):
    width = gated.shape[1]
    halo = near.shape[0]
    core = lax.axis_index("core")
    block = chain_block(core)
    ends = [lengths[0, 0]]
    for user in range(1, lengths.shape[1]):
        ends.append(ends[-1] + lengths[0, user])
    columns = MOST * TILE
    lane = lax.broadcasted_iota(jnp.int32, (TILE, columns), 1)
    row = lax.broadcasted_iota(jnp.int32, (TILE, columns), 0)
    causal = lane - (columns - TILE) <= row
    for r in range(2):
        tile = 2 * block + r
        start, end = jnp.int32(0), ends[-1]
        for stop in ends:
            start = jnp.maximum(start, jnp.where(stop <= tile, stop, 0))
            end = jnp.minimum(end, jnp.where(stop > tile, stop, ends[-1]))
        live = (lane // TILE + (tile - (MOST - 1)) >= start) & causal
        events = jnp.full((TILE, columns), (end - start) * TILE, jnp.int32).astype(F32)
        factor[r] = jnp.where(live, 1.0 / events, 0.0)

    def head_slices(h):
        at = pl.multiple_of(h * HEAD, HEAD)
        return [pl.ds(part * width + at, HEAD) for part in range(4)]

    def forward(h, carry):
        _, at_v, at_q, at_k = head_slices(h)
        near_v, near_k = pl.ds(pl.multiple_of(h * HEAD, HEAD), HEAD), head_slices(h)[1]
        keys = jnp.concatenate([near[:, near_k], proj[:, at_k]], axis=0)
        values = jnp.concatenate([near[:, near_v], proj[:, at_v]], axis=0)
        all_scores = dot_nt(proj[:, at_q], keys)
        for r in range(2):
            rows = slice(r * TILE, (r + 1) * TILE)
            window = slice(r * TILE, r * TILE + columns)
            scores = all_scores[rows, window]
            silu, bent = silu_pair(scores * (0.5 * SCALE))
            att = (silu * factor[r]).astype(BF16)
            att_all[h, r] = att
            bent_all[h, r] = (bent * factor[r]).astype(BF16)
            attended[rows, near_v] = dot_nn(att, values[window])
        return carry

    lax.fori_loop(0, HEADS, forward, 0, unroll=8)

    for r in range(2):
        rows = slice(r * TILE, (r + 1) * TILE)
        gate = proj[rows, 0:width].astype(F32)
        normal, recip = normalize(attended[rows, :])
        gated[rows, :] = (normal * gate).astype(BF16)
        upstream = d_gated[rows, :]
        d_attended[rows, :] = norm_back(upstream * gate, normal, recip).astype(BF16)
        d_pre[rows, 0:width] = (upstream * normal * slope[rows, 0:width].astype(F32)).astype(BF16)

    def backward(h, carry):
        _, at_v, at_q, at_k = head_slices(h)
        near_v, near_k = pl.ds(pl.multiple_of(h * HEAD, HEAD), HEAD), head_slices(h)[1]
        keys = jnp.concatenate([near[:, near_k], proj[:, at_k]], axis=0)
        values = jnp.concatenate([near[:, near_v], proj[:, at_v]], axis=0)
        blank = jnp.zeros((TILE, TILE), BF16)

        def spread(parts):
            return jnp.concatenate(
                [jnp.concatenate([parts[0], blank], axis=1), jnp.concatenate([blank, parts[1]], axis=1)], axis=0
            )

        queries, upstream = proj[:, at_q], d_attended[:, near_v]
        d_scores = []
        d_all = dot_nt(upstream, values)
        for r in range(2):
            rows = slice(r * TILE, (r + 1) * TILE)
            window = slice(r * TILE, r * TILE + columns)
            d_att = d_all[rows, window]
            d_scores.append((d_att * bent_all[h, r].astype(F32)).astype(BF16))
        d_scores = spread(d_scores)
        d_query = dot_nn(d_scores, keys) * SCALE
        d_pre[:, at_q] = (d_query * slope[:, at_q].astype(F32)).astype(BF16)
        d_key = dot_tn(d_scores, queries) * SCALE
        d_value = dot_tn(spread([att_all[h, 0], att_all[h, 1]]), upstream)
        for total, own_at, near_at in ((d_key, at_k, near_k), (d_value, at_v, near_v)):
            near_d_pre[:, near_at] = (
                total[:halo] * near_slope[:, near_at].astype(F32)
            ).astype(BF16)
            d_pre[:, own_at] = (total[halo:] * slope[:, own_at].astype(F32)).astype(BF16)
        return carry

    lax.fori_loop(0, HEADS, backward, 0, unroll=8)


def attention(lengths, proj, slope, near, near_slope, d_gated):
    rows, width = d_gated.shape
    halo = near.shape[0]
    shapes = [((rows, width), BF16), ((rows, 4 * width), BF16), ((halo, 2 * width), BF16)]
    return pl.pallas_call(
        attention_kernel,
        in_specs=[pl.BlockSpec(memory_space=pltpu.SMEM)] + [whole()] * 5,
        out_specs=[whole()] * 3,
        out_shape=[jax.ShapeDtypeStruct(*s) for s in shapes],
        scratch_shapes=[
            pltpu.VMEM((2, TILE, MOST * TILE), F32),
            pltpu.VMEM((HEADS, 2, TILE, MOST * TILE), BF16),
            pltpu.VMEM((HEADS, 2, TILE, MOST * TILE), BF16),
            pltpu.VMEM((rows, width), F32),
            pltpu.VMEM((rows, width), BF16),
        ],
        compiler_params=pltpu.CompilerParams(vmem_limit_bytes=SCOPED),
        cost_estimate=pl.CostEstimate(
            flops=2 * 800 * MIB, bytes_accessed=16 * MIB, transcendentals=MIB
        ),
    )(lengths, proj, slope, near, near_slope, d_gated)


def key_grad_kernel(near_normed, normed, near_d_pre, d_pre, send, keep):
    width = normed.shape[1]
    even = lax.axis_index("core") == 0
    half = width // 2
    side, depth = keep.shape[:2]
    d_key = jnp.concatenate([near_d_pre[:, width:], d_pre[:, 3 * width :]], axis=0)
    upper = lax.broadcasted_iota(jnp.int32, (1, 8, half), 1) < 4
    step = width // depth
    for z in range(depth):
        at = slice(z * step, (z + 1) * step)
        part = jnp.concatenate([near_normed[:, at], normed[:, at]], axis=0)
        grad = dot_tn(part, d_key).reshape(side * side, 8, width)
        left, right = grad[:, :, :half], grad[:, :, half:]
        first = jnp.where(upper, left, pltpu.roll(right, 4, 1))
        last = jnp.where(upper, pltpu.roll(left, 4, 1), right)
        kept = jnp.where(even, first, last).astype(BF16)
        sent = jnp.where(even, last, first).astype(BF16)
        for y in range(side):
            keep[y, z] = kept[y * side : (y + 1) * side]
            send[y, z] = sent[y * side : (y + 1) * side]


def key_grad(near_normed, normed, near_d_pre, d_pre):
    width = normed.shape[1]
    depth, side = lax.axis_size("dp"), lax.axis_size("x")
    shape = jax.ShapeDtypeStruct((side, depth, side, 8, width // 2), BF16)
    return pl.pallas_call(
        key_grad_kernel,
        in_specs=[whole()] * 4,
        out_specs=[whole()] * 2,
        out_shape=[shape, shape],
        compiler_params=pltpu.CompilerParams(vmem_limit_bytes=SCOPED),
        cost_estimate=TINY,
    )(near_normed, normed, near_d_pre, d_pre)


def ring_first_kernel(keep, received, total, up, down):
    place = lax.axis_index("y")
    half = up.shape[0]
    total[...] = (keep[...].astype(F32) + received[...].astype(F32)).astype(BF16)
    opposite = total.at[lax.rem(place + 2, 4)]
    up[...] = opposite[:half]
    down[...] = opposite[half:]


def ring_second_kernel(total, from_below, from_above, up, down):
    place = lax.axis_index("y")
    half = from_below.shape[0]
    above, below = total.at[lax.rem(place + 1, 4)], total.at[lax.rem(place + 3, 4)]
    up[:half] = (above[:half].astype(F32) + from_below[...].astype(F32)).astype(BF16)
    up[half:] = above[half:]
    down[:half] = below[:half]
    down[half:] = (below[half:].astype(F32) + from_above[...].astype(F32)).astype(BF16)


def ring_third_kernel(total, from_below, from_above, column):
    own = total.at[lax.axis_index("y")]
    column[...] = (
        own[...].astype(F32) + from_below[...].astype(F32) + from_above[...].astype(F32)
    ).astype(BF16)


def on_device(kernel, shapes, *arrays):
    return pl.pallas_call(
        kernel,
        in_specs=[whole()] * len(arrays),
        out_specs=[whole()] * len(shapes),
        out_shape=[jax.ShapeDtypeStruct(shape, BF16) for shape in shapes],
        compiler_params=pltpu.CompilerParams(vmem_limit_bytes=SCOPED),
        cost_estimate=TINY,
    )(*arrays)


def near_through_kernel(near_d_pre, weight, far, out):
    width = weight.shape[0]
    step = 256
    for n in range(0, width, step):
        at = slice(n, n + step)
        near = dot_nt(near_d_pre[:, :width], weight[at, width : 2 * width])
        near = (near + dot_nt(near_d_pre[:, width:], weight[at, 3 * width :])).astype(BF16)
        far[:, at] = near[:TILE]
        out[:, at] = near[TILE:]


def near_through(near_d_pre, weight):
    halo, width = near_d_pre.shape[0], weight.shape[0]
    return pl.pallas_call(
        near_through_kernel,
        in_specs=[whole()] * 2,
        out_specs=[whole()] * 2,
        out_shape=[
            jax.ShapeDtypeStruct((TILE, width), BF16), jax.ShapeDtypeStruct((halo - TILE, width), BF16)
        ],
        compiler_params=pltpu.CompilerParams(vmem_limit_bytes=SCOPED),
        cost_estimate=TINY,
    )(near_d_pre, weight)


def through_kernel(d_pre, gated, mine, second, weight, weight_out, d_normed, outs):
    width = weight.shape[0]
    step = 256
    for n in range(0, width, step):
        at = slice(n, n + step)
        d_normed[:, at] = dot_nt(d_pre[...], weight[at, :])
        update = dot_nn(gated[...], weight_out[:, at])
        outs[:TILE, at] = (mine[:, at].astype(F32) + update[:TILE]).astype(BF16)
        outs[TILE:, at] = (second[:, at].astype(F32) + update[TILE:]).astype(BF16)


def through(d_pre, gated, mine, second, weight, weight_out):
    rows, width = d_pre.shape[0], weight.shape[0]
    return pl.pallas_call(
        through_kernel,
        in_specs=[whole()] * 6,
        out_specs=[whole()] * 2,
        out_shape=[
            jax.ShapeDtypeStruct((rows, width), F32), jax.ShapeDtypeStruct((rows, width), BF16)
        ],
        compiler_params=pltpu.CompilerParams(vmem_limit_bytes=SCOPED),
        cost_estimate=TINY,
    )(d_pre, gated, mine, second, weight, weight_out)


def merge_kernel(d_normed, arrived, outs, own, given):
    own[...] = d_normed[:TILE, :] + arrived[:TILE, :].astype(F32)
    given[:TILE, :] = outs[TILE:, :]
    given[TILE:, :] = (d_normed[TILE:, :] + arrived[TILE:, :].astype(F32)).astype(BF16)


def merge(d_normed, arrived, outs):
    rows, width = outs.shape
    return pl.pallas_call(
        merge_kernel,
        in_specs=[whole()] * 3,
        out_specs=[whole()] * 2,
        out_shape=[
            jax.ShapeDtypeStruct((TILE, width), F32),
            jax.ShapeDtypeStruct((rows, width), BF16),
        ],
        compiler_params=pltpu.CompilerParams(vmem_limit_bytes=SCOPED),
        cost_estimate=TINY,
    )(d_normed, arrived, outs)


def finish_kernel(
    events, back, outs, own, taken, far, layer_out, event_grads, layer, grads, sems
):
    core = lax.axis_index("core")
    kept = pl.ds(pl.multiple_of(core * TILE, TILE), TILE)
    swapped = pl.ds(pl.multiple_of((1 - core) * TILE, TILE), TILE)
    layer[0] = outs[:TILE, :]
    layer[1] = taken[:TILE, :]
    stores = [
        pltpu.make_async_copy(layer.at[r], layer_out.at[rows], sems.at[r])
        for r, rows in enumerate((kept, swapped))
    ]
    for copy in stores:
        copy.start()
    sums = (
        (kept, own[...]),
        (swapped, taken[TILE:, :].astype(F32) + far[...].astype(F32)),
    )
    for r, (rows, d_normed) in enumerate(sums):
        normed_f, recip = normalize(events[rows, :].astype(F32))
        grads[r] = (back[rows, :].astype(F32) + norm_back(d_normed, normed_f, recip)).astype(BF16)
        stores.append(pltpu.make_async_copy(grads.at[r], event_grads.at[rows], sems.at[2 + r]))
        stores[-1].start()
    for copy in stores:
        copy.wait()


def finish(events, back, outs, own, taken, far):
    rows, width = events.shape
    return pl.pallas_call(
        finish_kernel,
        in_specs=[whole()] * 6,
        out_specs=[remote()] * 2,
        out_shape=[jax.ShapeDtypeStruct((rows, width), BF16)] * 2,
        scratch_shapes=[
            pltpu.VMEM((2, TILE, width), BF16),
            pltpu.VMEM((2, TILE, width), BF16),
            pltpu.SemaphoreType.DMA((4,)),
        ],
        compiler_params=pltpu.CompilerParams(vmem_limit_bytes=SCOPED),
        cost_estimate=pl.CostEstimate(flops=4 * MIB, bytes_accessed=4 * MIB, transcendentals=0),
    )(events, back, outs, own, taken, far)


def sum_kernel(parts, out):
    total = parts[0].astype(F32)
    for n in range(1, parts.shape[0]):
        total = total + parts[n].astype(F32)
    out[:, : total.shape[1]] = total[:4]
    out[:, total.shape[1] :] = total[4:]


def sum_parts(parts):
    return pl.pallas_call(
        sum_kernel,
        in_specs=[whole()],
        out_specs=whole(),
        out_shape=jax.ShapeDtypeStruct((4, 2 * parts.shape[-1]), F32),
        compiler_params=pltpu.CompilerParams(vmem_limit_bytes=SCOPED),
        cost_estimate=TINY,
    )(parts)


def around(block, shift):
    return lax.ppermute(block, "y", [(i, (i + shift) % 4) for i in range(4)])


def shards(events, lengths, weight_in, weight_out, cotangent):
    pairs = lax.axis_size(SEQ)
    onward, far_on, backward, far_back = routes(pairs)
    swap = [(i, i ^ 1) for i in range(pairs)]
    local = events.reshape(2 * TILE, -1)
    back = cotangent.reshape(2 * TILE, -1)

    mine, other = split(local)
    far = move(other, far_on)
    second = move(other, swap)
    back_mine, back_other = split(back)
    back_second = move(back_other, swap)
    normed = normalize_block(mine, second)
    near = move(normed, onward)

    far, normed = lax.optimization_barrier((far, normed))
    proj, slope, d_gated = project(normed, back_mine, back_second, weight_in, weight_out)
    far, near, proj = lax.optimization_barrier((far, near, proj))
    near_normed, near, near_slope = project_near(far, near, weight_in)
    gated, d_pre, near_d_pre = attention(lengths, proj, slope, near, near_slope, d_gated)

    tie = lax.optimization_barrier
    far_d, near_d = near_through(near_d_pre, weight_in)
    arrived = move(near_d, backward)
    near_d_pre, near_d = tie((near_d_pre, near_d))
    send, keep = key_grad(near_normed, normed, near_d_pre, d_pre)
    received = move(send, swap)

    block = keep.shape[1:]
    half = (block[0] // 2,) + block[1:]
    total, up, down = on_device(ring_first_kernel, [keep.shape, half, half], keep, received)
    from_below, from_above = around(up, 1), around(down, -1)
    far_d, d_pre, total = tie((far_d, d_pre, total))
    far_in = move(far_d, far_back)
    d_normed, outs = through(d_pre, gated, mine, second, weight_in, weight_out)
    from_below, from_above, d_normed, far_in = tie((from_below, from_above, d_normed, far_in))
    up, down = on_device(ring_second_kernel, [block, block], total, from_below, from_above)
    from_below, from_above = around(up, 1), around(down, -1)
    d_normed, up = tie((d_normed, up))
    own, given = merge(d_normed, arrived, outs)
    taken = move(given, swap)
    from_below, from_above, taken = tie((from_below, from_above, taken))
    (column,) = on_device(ring_third_kernel, [block], total, from_below, from_above)
    column = column.reshape((block[0] * block[1],) + block[2:])
    parts = lax.all_to_all(column, ("dp", "x"), split_axis=0, concat_axis=0, tiled=True)
    layer_out, event_grads = finish(local, back, outs, own, taken, far_in)
    summed = sum_parts(parts)
    return (layer_out.reshape(events.shape), event_grads.reshape(events.shape), summed)


def solution(mesh):
    devices = mesh.devices
    fine = Mesh(devices.reshape(devices.shape[0], 4, 4, 2), ("dp",) + SEQ)
    every = P("dp", SEQ, None, None)
    return jax.shard_map(
        shards,
        mesh=fine,
        in_specs=(every, P("dp", None), P(), P(), every),
        out_specs=(every, every, P(("dp",) + SEQ, None)),
        check_vma=False,
    )
```

```python
import jax
import jax.numpy as jnp
from jax import lax
from jax.experimental import pallas as pl
from jax.experimental.pallas import tpu as pltpu
from jax.sharding import Mesh, PartitionSpec as P

HEADS = 8
HEAD = 128
TILE = 128
MOST = 4
EPSILON = 1e-06
SCALE = HEAD ** (-0.5)
SEQ = ("y", "x", "core")
MIB = 1024 * 1024
SCOPED = 16 * MIB
TINY = pl.CostEstimate(flops=1024, bytes_accessed=1024, transcendentals=0)

F32 = jnp.float32
BF16 = jnp.bfloat16


def chain_device(block, chips):
    return 2 * block if block < chips else 2 * (2 * chips - 1 - block) + 1


def chain_block(core):
    pair = lax.axis_index(SEQ)
    return jnp.where(core == 0, pair // 2, lax.axis_size(SEQ) - 1 - pair // 2)


def tile_owner(tile, pairs):
    return tile if tile < pairs else 2 * pairs - 1 - tile


def routes(pairs):
    chips = pairs // 2
    place = [chain_device(block, chips) for block in range(pairs)]
    onward = [(place[b - 1], place[b]) for b in range(1, pairs)]
    far = [(tile_owner(2 * b - 3, pairs), place[b]) for b in range(2, pairs)]
    back = [(place[b], place[b - 1]) for b in range(1, pairs)]
    far_back = [(place[b], tile_owner(2 * b - 3, pairs)) for b in range(2, pairs)]
    return onward, far, back, far_back


def move(block, route):
    return lax.ppermute(block, SEQ, route)


def normalize(values):
    centre = jnp.mean(values, axis=-1, keepdims=True)
    centred = values - centre
    spread = jnp.mean(centred * centred, axis=-1, keepdims=True)
    recip = lax.rsqrt(spread + EPSILON)
    return centred * recip, recip


def norm_back(upstream, normed_f, recip):
    first = jnp.mean(upstream, axis=-1, keepdims=True)
    second = jnp.mean(upstream * normed_f, axis=-1, keepdims=True)
    return recip * (upstream - first - normed_f * second)


def silu_pair(half):
    rise = 1.0 + jnp.tanh(half)
    silu = half * rise
    return silu, rise * ((0.5 + half) - 0.5 * silu)


def dot_nn(left, right):
    return lax.dot_general(left, right, (((1,), (0,)), ((), ())), preferred_element_type=F32)


def dot_nt(left, right):
    return lax.dot_general(left, right, (((1,), (1,)), ((), ())), preferred_element_type=F32)


def dot_tn(left, right):
    return lax.dot_general(left, right, (((0,), (0,)), ((), ())), preferred_element_type=F32)


def whole():
    return pl.BlockSpec(memory_space=pltpu.VMEM)


def remote():
    return pl.BlockSpec(memory_space=pltpu.HBM)


def split_kernel(array, mine, other, sems):
    core = lax.axis_index("core")
    copies = [
        pltpu.make_async_copy(array.at[pl.ds(pl.multiple_of(at * TILE, TILE), TILE)], out, sems.at[n])
        for n, (at, out) in enumerate(((1 - core, other), (core, mine)))
    ]
    for copy in copies:
        copy.start()
    for copy in copies:
        copy.wait()


def split(array):
    tile = jax.ShapeDtypeStruct((TILE, array.shape[1]), BF16)
    return pl.pallas_call(
        split_kernel,
        in_specs=[remote()],
        out_specs=[whole()] * 2,
        out_shape=[tile, tile],
        scratch_shapes=[pltpu.SemaphoreType.DMA((2,))],
        compiler_params=pltpu.CompilerParams(vmem_limit_bytes=2 * MIB),
        cost_estimate=pl.CostEstimate(flops=8 * 1024 * MIB, bytes_accessed=24 * MIB, transcendentals=0),
    )(array)


def project_columns(normed, weight, columns, proj, slope):
    step = 512
    for n, at in enumerate(columns):
        pre = dot_nn(normed[...], weight[:, at : at + step])
        silu, bent = silu_pair(0.5 * pre)
        proj[:, n * step : (n + 1) * step] = silu.astype(BF16)
        slope[:, n * step : (n + 1) * step] = bent.astype(BF16)


def normalize_kernel(mine, second, normed):
    for r, tile in enumerate((mine, second)):
        rows = slice(r * TILE, (r + 1) * TILE)
        normed[rows, :] = normalize(tile[...].astype(F32))[0].astype(BF16)


def normalize_block(mine, second):
    rows, width = mine.shape
    return pl.pallas_call(
        normalize_kernel,
        in_specs=[whole()] * 2,
        out_specs=whole(),
        out_shape=jax.ShapeDtypeStruct((2 * rows, width), BF16),
        compiler_params=pltpu.CompilerParams(vmem_limit_bytes=2 * MIB),
        cost_estimate=pl.CostEstimate(flops=1024 * MIB, bytes_accessed=MIB, transcendentals=0),
    )(mine, second)


def project_kernel(normed, back_mine, back_second, weight_in, weight_out, proj, slope, d_gated):
    width = weight_in.shape[0]
    project_columns(normed, weight_in, range(0, 4 * width, 512), proj, slope)
    for n in range(0, width, 256):
        part = weight_out[n : n + 256, :]
        d_gated[:TILE, n : n + 256] = dot_nt(back_mine[...], part)
        d_gated[TILE:, n : n + 256] = dot_nt(back_second[...], part)


def project(normed, back_mine, back_second, weight, weight_out):
    width, columns = weight.shape
    rows = 2 * TILE
    shapes = [((rows, columns), BF16), ((rows, columns), BF16), ((rows, width), F32)]
    return pl.pallas_call(
        project_kernel,
        in_specs=[whole()] * 5,
        out_specs=[whole()] * 3,
        out_shape=[jax.ShapeDtypeStruct(*s) for s in shapes],
        compiler_params=pltpu.CompilerParams(vmem_limit_bytes=SCOPED),
        cost_estimate=pl.CostEstimate(
            flops=2 * rows * width * (columns + width),
            bytes_accessed=2 * (width * columns + 2 * rows * columns),
            transcendentals=rows * columns,
        ),
    )(normed, back_mine, back_second, weight, weight_out)


def project_near_kernel(far, near, weight, normed, proj, slope):
    width = weight.shape[0]
    normed[:TILE, :] = normalize(far[...].astype(F32))[0].astype(BF16)
    normed[TILE:, :] = near[...]
    columns = [part * width + at for part in (1, 3) for at in range(0, width, 512)]
    project_columns(normed, weight, columns, proj, slope)


def project_near(far, near, weight):
    rows, width = 3 * TILE, weight.shape[0]
    shapes = [((rows, width), BF16), ((rows, 2 * width), BF16), ((rows, 2 * width), BF16)]
    return pl.pallas_call(
        project_near_kernel,
        in_specs=[whole()] * 3,
        out_specs=[whole()] * 3,
        out_shape=[jax.ShapeDtypeStruct(*s) for s in shapes],
        compiler_params=pltpu.CompilerParams(vmem_limit_bytes=SCOPED),
        cost_estimate=pl.CostEstimate(
            flops=4 * rows * width * width, bytes_accessed=8 * width * width, transcendentals=2 * rows * width
        ),
    )(far, near, weight)


def attention_kernel(
    lengths, proj, slope, near, near_slope, d_gated,
    gated, d_pre, near_d_pre,
    factor, att_all, bent_all, attended, d_attended,
):
    width = gated.shape[1]
    halo = near.shape[0]
    core = lax.axis_index("core")
    block = chain_block(core)
    ends = [lengths[0, 0]]
    for user in range(1, lengths.shape[1]):
        ends.append(ends[-1] + lengths[0, user])
    columns = MOST * TILE
    lane = lax.broadcasted_iota(jnp.int32, (TILE, columns), 1)
    row = lax.broadcasted_iota(jnp.int32, (TILE, columns), 0)
    causal = lane - (columns - TILE) <= row
    for r in range(2):
        tile = 2 * block + r
        start, end = jnp.int32(0), ends[-1]
        for stop in ends:
            start = jnp.maximum(start, jnp.where(stop <= tile, stop, 0))
            end = jnp.minimum(end, jnp.where(stop > tile, stop, ends[-1]))
        live = (lane // TILE + (tile - (MOST - 1)) >= start) & causal
        events = jnp.full((TILE, columns), (end - start) * TILE, jnp.int32).astype(F32)
        factor[r] = jnp.where(live, 1.0 / events, 0.0)

    def head_slices(h):
        at = pl.multiple_of(h * HEAD, HEAD)
        return [pl.ds(part * width + at, HEAD) for part in range(4)]

    def forward(h, carry):
        _, at_v, at_q, at_k = head_slices(h)
        near_v, near_k = pl.ds(pl.multiple_of(h * HEAD, HEAD), HEAD), head_slices(h)[1]
        keys = jnp.concatenate([near[:, near_k], proj[:, at_k]], axis=0)
        values = jnp.concatenate([near[:, near_v], proj[:, at_v]], axis=0)
        all_scores = dot_nt(proj[:, at_q], keys)
        for r in range(2):
            rows = slice(r * TILE, (r + 1) * TILE)
            window = slice(r * TILE, r * TILE + columns)
            scores = all_scores[rows, window]
            silu, bent = silu_pair(scores * (0.5 * SCALE))
            att = (silu * factor[r]).astype(BF16)
            att_all[h, r] = att
            bent_all[h, r] = (bent * factor[r]).astype(BF16)
            attended[rows, near_v] = dot_nn(att, values[window])
        return carry

    lax.fori_loop(0, HEADS, forward, 0, unroll=8)

    for r in range(2):
        rows = slice(r * TILE, (r + 1) * TILE)
        gate = proj[rows, 0:width].astype(F32)
        normal, recip = normalize(attended[rows, :])
        gated[rows, :] = (normal * gate).astype(BF16)
        upstream = d_gated[rows, :]
        d_attended[rows, :] = norm_back(upstream * gate, normal, recip).astype(BF16)
        d_pre[rows, 0:width] = (upstream * normal * slope[rows, 0:width].astype(F32)).astype(BF16)

    def backward(h, carry):
        _, at_v, at_q, at_k = head_slices(h)
        near_v, near_k = pl.ds(pl.multiple_of(h * HEAD, HEAD), HEAD), head_slices(h)[1]
        keys = jnp.concatenate([near[:, near_k], proj[:, at_k]], axis=0)
        values = jnp.concatenate([near[:, near_v], proj[:, at_v]], axis=0)
        blank = jnp.zeros((TILE, TILE), BF16)

        def spread(parts):
            return jnp.concatenate(
                [jnp.concatenate([parts[0], blank], axis=1), jnp.concatenate([blank, parts[1]], axis=1)], axis=0
            )

        queries, upstream = proj[:, at_q], d_attended[:, near_v]
        d_scores = []
        d_all = dot_nt(upstream, values)
        for r in range(2):
            rows = slice(r * TILE, (r + 1) * TILE)
            window = slice(r * TILE, r * TILE + columns)
            d_att = d_all[rows, window]
            d_scores.append((d_att * bent_all[h, r].astype(F32)).astype(BF16))
        d_scores = spread(d_scores)
        d_query = dot_nn(d_scores, keys) * SCALE
        d_pre[:, at_q] = (d_query * slope[:, at_q].astype(F32)).astype(BF16)
        d_key = dot_tn(d_scores, queries) * SCALE
        d_value = dot_tn(spread([att_all[h, 0], att_all[h, 1]]), upstream)
        for total, own_at, near_at in ((d_key, at_k, near_k), (d_value, at_v, near_v)):
            near_d_pre[:, near_at] = (
                total[:halo] * near_slope[:, near_at].astype(F32)
            ).astype(BF16)
            d_pre[:, own_at] = (total[halo:] * slope[:, own_at].astype(F32)).astype(BF16)
        return carry

    lax.fori_loop(0, HEADS, backward, 0, unroll=8)


def attention(lengths, proj, slope, near, near_slope, d_gated):
    rows, width = d_gated.shape
    halo = near.shape[0]
    shapes = [((rows, width), BF16), ((rows, 4 * width), BF16), ((halo, 2 * width), BF16)]
    return pl.pallas_call(
        attention_kernel,
        in_specs=[pl.BlockSpec(memory_space=pltpu.SMEM)] + [whole()] * 5,
        out_specs=[whole()] * 3,
        out_shape=[jax.ShapeDtypeStruct(*s) for s in shapes],
        scratch_shapes=[
            pltpu.VMEM((2, TILE, MOST * TILE), F32),
            pltpu.VMEM((HEADS, 2, TILE, MOST * TILE), BF16),
            pltpu.VMEM((HEADS, 2, TILE, MOST * TILE), BF16),
            pltpu.VMEM((rows, width), F32),
            pltpu.VMEM((rows, width), BF16),
        ],
        compiler_params=pltpu.CompilerParams(vmem_limit_bytes=SCOPED),
        cost_estimate=pl.CostEstimate(
            flops=2 * 800 * MIB, bytes_accessed=16 * MIB, transcendentals=MIB
        ),
    )(lengths, proj, slope, near, near_slope, d_gated)


def key_grad_kernel(near_normed, normed, near_d_pre, d_pre, send, keep):
    width = normed.shape[1]
    even = lax.axis_index("core") == 0
    half = width // 2
    side, depth = keep.shape[:2]
    d_key = jnp.concatenate([near_d_pre[:, width:], d_pre[:, 3 * width :]], axis=0)
    upper = lax.broadcasted_iota(jnp.int32, (1, 8, half), 1) < 4
    step = width // depth
    for z in range(depth):
        at = slice(z * step, (z + 1) * step)
        part = jnp.concatenate([near_normed[:, at], normed[:, at]], axis=0)
        grad = dot_tn(part, d_key).reshape(side * side, 8, width)
        left, right = grad[:, :, :half], grad[:, :, half:]
        first = jnp.where(upper, left, pltpu.roll(right, 4, 1))
        last = jnp.where(upper, pltpu.roll(left, 4, 1), right)
        kept = jnp.where(even, first, last).astype(BF16)
        sent = jnp.where(even, last, first).astype(BF16)
        for y in range(side):
            keep[y, z] = kept[y * side : (y + 1) * side]
            send[y, z] = sent[y * side : (y + 1) * side]


def key_grad(near_normed, normed, near_d_pre, d_pre):
    width = normed.shape[1]
    depth, side = lax.axis_size("dp"), lax.axis_size("x")
    shape = jax.ShapeDtypeStruct((side, depth, side, 8, width // 2), BF16)
    return pl.pallas_call(
        key_grad_kernel,
        in_specs=[whole()] * 4,
        out_specs=[whole()] * 2,
        out_shape=[shape, shape],
        compiler_params=pltpu.CompilerParams(vmem_limit_bytes=SCOPED),
        cost_estimate=TINY,
    )(near_normed, normed, near_d_pre, d_pre)


def ring_first_kernel(keep, received, total, up, down):
    place = lax.axis_index("y")
    half = up.shape[0]
    total[...] = (keep[...].astype(F32) + received[...].astype(F32)).astype(BF16)
    opposite = total.at[lax.rem(place + 2, 4)]
    up[...] = opposite[:half]
    down[...] = opposite[half:]


def ring_second_kernel(total, from_below, from_above, up, down):
    place = lax.axis_index("y")
    half = from_below.shape[0]
    above, below = total.at[lax.rem(place + 1, 4)], total.at[lax.rem(place + 3, 4)]
    up[:half] = (above[:half].astype(F32) + from_below[...].astype(F32)).astype(BF16)
    up[half:] = above[half:]
    down[:half] = below[:half]
    down[half:] = (below[half:].astype(F32) + from_above[...].astype(F32)).astype(BF16)


def ring_third_kernel(total, from_below, from_above, column):
    own = total.at[lax.axis_index("y")]
    column[...] = (
        own[...].astype(F32) + from_below[...].astype(F32) + from_above[...].astype(F32)
    ).astype(BF16)


def on_device(kernel, shapes, *arrays):
    return pl.pallas_call(
        kernel,
        in_specs=[whole()] * len(arrays),
        out_specs=[whole()] * len(shapes),
        out_shape=[jax.ShapeDtypeStruct(shape, BF16) for shape in shapes],
        compiler_params=pltpu.CompilerParams(vmem_limit_bytes=SCOPED),
        cost_estimate=TINY,
    )(*arrays)


def near_through_kernel(near_d_pre, weight, far, out):
    width = weight.shape[0]
    step = 256
    for n in range(0, width, step):
        at = slice(n, n + step)
        near = dot_nt(near_d_pre[:, :width], weight[at, width : 2 * width])
        near = (near + dot_nt(near_d_pre[:, width:], weight[at, 3 * width :])).astype(BF16)
        far[:, at] = near[:TILE]
        out[:, at] = near[TILE:]


def near_through(near_d_pre, weight):
    halo, width = near_d_pre.shape[0], weight.shape[0]
    return pl.pallas_call(
        near_through_kernel,
        in_specs=[whole()] * 2,
        out_specs=[whole()] * 2,
        out_shape=[
            jax.ShapeDtypeStruct((TILE, width), BF16), jax.ShapeDtypeStruct((halo - TILE, width), BF16)
        ],
        compiler_params=pltpu.CompilerParams(vmem_limit_bytes=SCOPED),
        cost_estimate=TINY,
    )(near_d_pre, weight)


def through_kernel(d_pre, gated, mine, second, weight, weight_out, d_normed, outs):
    width = weight.shape[0]
    step = 256
    for n in range(0, width, step):
        at = slice(n, n + step)
        d_normed[:, at] = dot_nt(d_pre[...], weight[at, :])
        update = dot_nn(gated[...], weight_out[:, at])
        outs[:TILE, at] = (mine[:, at].astype(F32) + update[:TILE]).astype(BF16)
        outs[TILE:, at] = (second[:, at].astype(F32) + update[TILE:]).astype(BF16)


def through(d_pre, gated, mine, second, weight, weight_out):
    rows, width = d_pre.shape[0], weight.shape[0]
    return pl.pallas_call(
        through_kernel,
        in_specs=[whole()] * 6,
        out_specs=[whole()] * 2,
        out_shape=[
            jax.ShapeDtypeStruct((rows, width), F32), jax.ShapeDtypeStruct((rows, width), BF16)
        ],
        compiler_params=pltpu.CompilerParams(vmem_limit_bytes=SCOPED),
        cost_estimate=TINY,
    )(d_pre, gated, mine, second, weight, weight_out)


def merge_kernel(d_normed, arrived, outs, own, given):
    own[...] = d_normed[:TILE, :] + arrived[:TILE, :].astype(F32)
    given[:TILE, :] = outs[TILE:, :]
    given[TILE:, :] = (d_normed[TILE:, :] + arrived[TILE:, :].astype(F32)).astype(BF16)


def merge(d_normed, arrived, outs):
    rows, width = outs.shape
    return pl.pallas_call(
        merge_kernel,
        in_specs=[whole()] * 3,
        out_specs=[whole()] * 2,
        out_shape=[
            jax.ShapeDtypeStruct((TILE, width), F32),
            jax.ShapeDtypeStruct((rows, width), BF16),
        ],
        compiler_params=pltpu.CompilerParams(vmem_limit_bytes=SCOPED),
        cost_estimate=TINY,
    )(d_normed, arrived, outs)


def finish_kernel(
    events, back, outs, own, taken, far, layer_out, event_grads, layer, grads, sems
):
    core = lax.axis_index("core")
    kept = pl.ds(pl.multiple_of(core * TILE, TILE), TILE)
    swapped = pl.ds(pl.multiple_of((1 - core) * TILE, TILE), TILE)
    layer[0] = outs[:TILE, :]
    layer[1] = taken[:TILE, :]
    stores = [
        pltpu.make_async_copy(layer.at[r], layer_out.at[rows], sems.at[r])
        for r, rows in enumerate((kept, swapped))
    ]
    for copy in stores:
        copy.start()
    sums = (
        (kept, own[...]),
        (swapped, taken[TILE:, :].astype(F32) + far[...].astype(F32)),
    )
    for r, (rows, d_normed) in enumerate(sums):
        normed_f, recip = normalize(events[rows, :].astype(F32))
        grads[r] = (back[rows, :].astype(F32) + norm_back(d_normed, normed_f, recip)).astype(BF16)
        stores.append(pltpu.make_async_copy(grads.at[r], event_grads.at[rows], sems.at[2 + r]))
        stores[-1].start()
    for copy in stores:
        copy.wait()


def finish(events, back, outs, own, taken, far):
    rows, width = events.shape
    return pl.pallas_call(
        finish_kernel,
        in_specs=[whole()] * 6,
        out_specs=[remote()] * 2,
        out_shape=[jax.ShapeDtypeStruct((rows, width), BF16)] * 2,
        scratch_shapes=[
            pltpu.VMEM((2, TILE, width), BF16),
            pltpu.VMEM((2, TILE, width), BF16),
            pltpu.SemaphoreType.DMA((4,)),
        ],
        compiler_params=pltpu.CompilerParams(vmem_limit_bytes=SCOPED),
        cost_estimate=pl.CostEstimate(flops=4 * MIB, bytes_accessed=4 * MIB, transcendentals=0),
    )(events, back, outs, own, taken, far)


def sum_kernel(parts, out):
    total = parts[0].astype(F32)
    for n in range(1, parts.shape[0]):
        total = total + parts[n].astype(F32)
    out[:, : total.shape[1]] = total[:4]
    out[:, total.shape[1] :] = total[4:]


def sum_parts(parts):
    return pl.pallas_call(
        sum_kernel,
        in_specs=[whole()],
        out_specs=whole(),
        out_shape=jax.ShapeDtypeStruct((4, 2 * parts.shape[-1]), F32),
        compiler_params=pltpu.CompilerParams(vmem_limit_bytes=SCOPED),
        cost_estimate=TINY,
    )(parts)


def around(block, shift):
    return lax.ppermute(block, "y", [(i, (i + shift) % 4) for i in range(4)])


def shards(events, lengths, weight_in, weight_out, cotangent):
    pairs = lax.axis_size(SEQ)
    onward, far_on, backward, far_back = routes(pairs)
    swap = [(i, i ^ 1) for i in range(pairs)]
    local = events.reshape(2 * TILE, -1)
    back = cotangent.reshape(2 * TILE, -1)

    mine, other = split(local)
    far = move(other, far_on)
    second = move(other, swap)
    back_mine, back_other = split(back)
    back_second = move(back_other, swap)
    normed = normalize_block(mine, second)
    near = move(normed, onward)

    far, normed = lax.optimization_barrier((far, normed))
    proj, slope, d_gated = project(normed, back_mine, back_second, weight_in, weight_out)
    far, near, proj = lax.optimization_barrier((far, near, proj))
    near_normed, near, near_slope = project_near(far, near, weight_in)
    gated, d_pre, near_d_pre = attention(lengths, proj, slope, near, near_slope, d_gated)

    tie = lax.optimization_barrier
    send, keep = key_grad(near_normed, normed, near_d_pre, d_pre)
    received = move(send, swap)
    near_d_pre, send = tie((near_d_pre, send))
    far_d, near_d = near_through(near_d_pre, weight_in)
    received, near_d = tie((received, near_d))

    block = keep.shape[1:]
    half = (block[0] // 2,) + block[1:]
    total, up, down = on_device(ring_first_kernel, [keep.shape, half, half], keep, received)
    from_below, from_above = around(up, 1), around(down, -1)
    d_pre, total = tie((d_pre, total))
    d_normed, outs = through(d_pre, gated, mine, second, weight_in, weight_out)
    from_below, from_above, d_normed, near_d, far_d = tie((from_below, from_above, d_normed, near_d, far_d))
    arrived = move(near_d, backward)
    far_in = move(far_d, far_back)
    up, down = on_device(ring_second_kernel, [block, block], total, from_below, from_above)
    from_below, from_above = around(up, 1), around(down, -1)
    from_below, from_above, arrived, far_in = tie((from_below, from_above, arrived, far_in))
    own, given = merge(d_normed, arrived, outs)
    taken = move(given, swap)
    from_below, own = tie((from_below, own))
    (column,) = on_device(ring_third_kernel, [block], total, from_below, from_above)
    column, taken = tie((column, taken))
    column = column.reshape((block[0] * block[1],) + block[2:])
    parts = lax.all_to_all(column, ("dp", "x"), split_axis=0, concat_axis=0, tiled=True)
    layer_out, event_grads = finish(local, back, outs, own, taken, far_in)
    summed = sum_parts(parts)
    return (layer_out.reshape(events.shape), event_grads.reshape(events.shape), summed)


def solution(mesh):
    devices = mesh.devices
    fine = Mesh(devices.reshape(devices.shape[0], 4, 4, 2), ("dp",) + SEQ)
    every = P("dp", SEQ, None, None)
    return jax.shard_map(
        shards,
        mesh=fine,
        in_specs=(every, P("dp", None), P(), P(), every),
        out_specs=(every, every, P(("dp",) + SEQ, None)),
        check_vma=False,
    )
```

```python
import jax
import jax.numpy as jnp
from jax import lax
from jax.experimental import pallas as pl
from jax.experimental.pallas import tpu as pltpu
from jax.sharding import Mesh, PartitionSpec as P

HEADS = 8
HEAD = 128
TILE = 128
MOST = 4
EPSILON = 1e-06
SCALE = HEAD ** (-0.5)
SEQ = ("y", "x", "core")
MIB = 1024 * 1024
SCOPED = 16 * MIB
TINY = pl.CostEstimate(flops=1024, bytes_accessed=1024, transcendentals=0)

F32 = jnp.float32
BF16 = jnp.bfloat16


def chain_device(block, chips):
    return 2 * block if block < chips else 2 * (2 * chips - 1 - block) + 1


def chain_block(core):
    pair = lax.axis_index(SEQ)
    return jnp.where(core == 0, pair // 2, lax.axis_size(SEQ) - 1 - pair // 2)


def tile_owner(tile, pairs):
    return tile if tile < pairs else 2 * pairs - 1 - tile


def routes(pairs):
    chips = pairs // 2
    place = [chain_device(block, chips) for block in range(pairs)]
    onward = [(place[b - 1], place[b]) for b in range(1, pairs)]
    far = [(tile_owner(2 * b - 3, pairs), place[b]) for b in range(2, pairs)]
    back = [(place[b], place[b - 1]) for b in range(1, pairs)]
    far_back = [(place[b], tile_owner(2 * b - 3, pairs)) for b in range(2, pairs)]
    return onward, far, back, far_back


def move(block, route):
    return lax.ppermute(block, SEQ, route)


def normalize(values):
    centre = jnp.mean(values, axis=-1, keepdims=True)
    centred = values - centre
    spread = jnp.mean(centred * centred, axis=-1, keepdims=True)
    recip = lax.rsqrt(spread + EPSILON)
    return centred * recip, recip


def norm_back(upstream, normed_f, recip):
    first = jnp.mean(upstream, axis=-1, keepdims=True)
    second = jnp.mean(upstream * normed_f, axis=-1, keepdims=True)
    return recip * (upstream - first - normed_f * second)


def silu_pair(half):
    rise = 1.0 + jnp.tanh(half)
    silu = half * rise
    return silu, rise * ((0.5 + half) - 0.5 * silu)


def dot_nn(left, right):
    return lax.dot_general(left, right, (((1,), (0,)), ((), ())), preferred_element_type=F32)


def dot_nt(left, right):
    return lax.dot_general(left, right, (((1,), (1,)), ((), ())), preferred_element_type=F32)


def dot_tn(left, right):
    return lax.dot_general(left, right, (((0,), (0,)), ((), ())), preferred_element_type=F32)


def whole():
    return pl.BlockSpec(memory_space=pltpu.VMEM)


def remote():
    return pl.BlockSpec(memory_space=pltpu.HBM)


def split_kernel(array, mine, other, sems):
    core = lax.axis_index("core")
    copies = [
        pltpu.make_async_copy(array.at[pl.ds(pl.multiple_of(at * TILE, TILE), TILE)], out, sems.at[n])
        for n, (at, out) in enumerate(((1 - core, other), (core, mine)))
    ]
    for copy in copies:
        copy.start()
    for copy in copies:
        copy.wait()


def split(array):
    tile = jax.ShapeDtypeStruct((TILE, array.shape[1]), BF16)
    return pl.pallas_call(
        split_kernel,
        in_specs=[remote()],
        out_specs=[whole()] * 2,
        out_shape=[tile, tile],
        scratch_shapes=[pltpu.SemaphoreType.DMA((2,))],
        compiler_params=pltpu.CompilerParams(vmem_limit_bytes=2 * MIB),
        cost_estimate=pl.CostEstimate(flops=8 * 1024 * MIB, bytes_accessed=24 * MIB, transcendentals=0),
    )(array)


def project_columns(normed, weight, columns, proj, slope):
    step = 512
    for n, at in enumerate(columns):
        pre = dot_nn(normed[...], weight[:, at : at + step])
        silu, bent = silu_pair(0.5 * pre)
        proj[:, n * step : (n + 1) * step] = silu.astype(BF16)
        slope[:, n * step : (n + 1) * step] = bent.astype(BF16)


def normalize_kernel(mine, second, normed):
    for r, tile in enumerate((mine, second)):
        rows = slice(r * TILE, (r + 1) * TILE)
        normed[rows, :] = normalize(tile[...].astype(F32))[0].astype(BF16)


def normalize_block(mine, second):
    rows, width = mine.shape
    return pl.pallas_call(
        normalize_kernel,
        in_specs=[whole()] * 2,
        out_specs=whole(),
        out_shape=jax.ShapeDtypeStruct((2 * rows, width), BF16),
        compiler_params=pltpu.CompilerParams(vmem_limit_bytes=2 * MIB),
        cost_estimate=pl.CostEstimate(flops=1024 * MIB, bytes_accessed=MIB, transcendentals=0),
    )(mine, second)


def project_kernel(normed, back_mine, back_second, weight_in, weight_out, proj, slope, d_gated):
    width = weight_in.shape[0]
    project_columns(normed, weight_in, range(0, 4 * width, 512), proj, slope)
    for n in range(0, width, 256):
        part = weight_out[n : n + 256, :]
        d_gated[:TILE, n : n + 256] = dot_nt(back_mine[...], part)
        d_gated[TILE:, n : n + 256] = dot_nt(back_second[...], part)


def project(normed, back_mine, back_second, weight, weight_out):
    width, columns = weight.shape
    rows = 2 * TILE
    shapes = [((rows, columns), BF16), ((rows, columns), BF16), ((rows, width), F32)]
    return pl.pallas_call(
        project_kernel,
        in_specs=[whole()] * 5,
        out_specs=[whole()] * 3,
        out_shape=[jax.ShapeDtypeStruct(*s) for s in shapes],
        compiler_params=pltpu.CompilerParams(vmem_limit_bytes=SCOPED),
        cost_estimate=pl.CostEstimate(
            flops=2 * rows * width * (columns + width),
            bytes_accessed=2 * (width * columns + 2 * rows * columns),
            transcendentals=rows * columns,
        ),
    )(normed, back_mine, back_second, weight, weight_out)


def project_near_kernel(far, near, weight, normed, proj, slope):
    width = weight.shape[0]
    normed[:TILE, :] = normalize(far[...].astype(F32))[0].astype(BF16)
    normed[TILE:, :] = near[...]
    columns = [part * width + at for part in (1, 3) for at in range(0, width, 512)]
    project_columns(normed, weight, columns, proj, slope)


def project_near(far, near, weight):
    rows, width = 3 * TILE, weight.shape[0]
    shapes = [((rows, width), BF16), ((rows, 2 * width), BF16), ((rows, 2 * width), BF16)]
    return pl.pallas_call(
        project_near_kernel,
        in_specs=[whole()] * 3,
        out_specs=[whole()] * 3,
        out_shape=[jax.ShapeDtypeStruct(*s) for s in shapes],
        compiler_params=pltpu.CompilerParams(vmem_limit_bytes=SCOPED),
        cost_estimate=pl.CostEstimate(
            flops=4 * rows * width * width, bytes_accessed=8 * width * width, transcendentals=2 * rows * width
        ),
    )(far, near, weight)


def attention_kernel(
    lengths, proj, slope, near, near_slope, d_gated,
    gated, d_pre, near_d_pre,
    factor, att_all, bent_all, attended, d_attended,
):
    width = gated.shape[1]
    halo = near.shape[0]
    core = lax.axis_index("core")
    block = chain_block(core)
    ends = [lengths[0, 0]]
    for user in range(1, lengths.shape[1]):
        ends.append(ends[-1] + lengths[0, user])
    columns = MOST * TILE
    lane = lax.broadcasted_iota(jnp.int32, (TILE, columns), 1)
    row = lax.broadcasted_iota(jnp.int32, (TILE, columns), 0)
    causal = lane - (columns - TILE) <= row
    for r in range(2):
        tile = 2 * block + r
        start, end = jnp.int32(0), ends[-1]
        for stop in ends:
            start = jnp.maximum(start, jnp.where(stop <= tile, stop, 0))
            end = jnp.minimum(end, jnp.where(stop > tile, stop, ends[-1]))
        live = (lane // TILE + (tile - (MOST - 1)) >= start) & causal
        events = jnp.full((TILE, columns), (end - start) * TILE, jnp.int32).astype(F32)
        factor[r] = jnp.where(live, 1.0 / events, 0.0)

    def head_slices(h):
        at = pl.multiple_of(h * HEAD, HEAD)
        return [pl.ds(part * width + at, HEAD) for part in range(4)]

    def forward(h, carry):
        _, at_v, at_q, at_k = head_slices(h)
        near_v, near_k = pl.ds(pl.multiple_of(h * HEAD, HEAD), HEAD), head_slices(h)[1]
        keys = jnp.concatenate([near[:, near_k], proj[:, at_k]], axis=0)
        values = jnp.concatenate([near[:, near_v], proj[:, at_v]], axis=0)
        all_scores = dot_nt(proj[:, at_q], keys)
        for r in range(2):
            rows = slice(r * TILE, (r + 1) * TILE)
            window = slice(r * TILE, r * TILE + columns)
            scores = all_scores[rows, window]
            silu, bent = silu_pair(scores * (0.5 * SCALE))
            att = (silu * factor[r]).astype(BF16)
            att_all[h, r] = att
            bent_all[h, r] = (bent * factor[r]).astype(BF16)
            attended[rows, near_v] = dot_nn(att, values[window])
        return carry

    lax.fori_loop(0, HEADS, forward, 0, unroll=8)

    for r in range(2):
        rows = slice(r * TILE, (r + 1) * TILE)
        gate = proj[rows, 0:width].astype(F32)
        normal, recip = normalize(attended[rows, :])
        gated[rows, :] = (normal * gate).astype(BF16)
        upstream = d_gated[rows, :]
        d_attended[rows, :] = norm_back(upstream * gate, normal, recip).astype(BF16)
        d_pre[rows, 0:width] = (upstream * normal * slope[rows, 0:width].astype(F32)).astype(BF16)

    def backward(h, carry):
        _, at_v, at_q, at_k = head_slices(h)
        near_v, near_k = pl.ds(pl.multiple_of(h * HEAD, HEAD), HEAD), head_slices(h)[1]
        keys = jnp.concatenate([near[:, near_k], proj[:, at_k]], axis=0)
        values = jnp.concatenate([near[:, near_v], proj[:, at_v]], axis=0)
        blank = jnp.zeros((TILE, TILE), BF16)

        def spread(parts):
            return jnp.concatenate(
                [jnp.concatenate([parts[0], blank], axis=1), jnp.concatenate([blank, parts[1]], axis=1)], axis=0
            )

        queries, upstream = proj[:, at_q], d_attended[:, near_v]
        d_scores = []
        d_all = dot_nt(upstream, values)
        for r in range(2):
            rows = slice(r * TILE, (r + 1) * TILE)
            window = slice(r * TILE, r * TILE + columns)
            d_att = d_all[rows, window]
            d_scores.append((d_att * bent_all[h, r].astype(F32)).astype(BF16))
        d_scores = spread(d_scores)
        d_query = dot_nn(d_scores, keys) * SCALE
        d_pre[:, at_q] = (d_query * slope[:, at_q].astype(F32)).astype(BF16)
        d_key = dot_tn(d_scores, queries) * SCALE
        d_value = dot_tn(spread([att_all[h, 0], att_all[h, 1]]), upstream)
        for total, own_at, near_at in ((d_key, at_k, near_k), (d_value, at_v, near_v)):
            near_d_pre[:, near_at] = (
                total[:halo] * near_slope[:, near_at].astype(F32)
            ).astype(BF16)
            d_pre[:, own_at] = (total[halo:] * slope[:, own_at].astype(F32)).astype(BF16)
        return carry

    lax.fori_loop(0, HEADS, backward, 0, unroll=8)


def attention(lengths, proj, slope, near, near_slope, d_gated):
    rows, width = d_gated.shape
    halo = near.shape[0]
    shapes = [((rows, width), BF16), ((rows, 4 * width), BF16), ((halo, 2 * width), BF16)]
    return pl.pallas_call(
        attention_kernel,
        in_specs=[pl.BlockSpec(memory_space=pltpu.SMEM)] + [whole()] * 5,
        out_specs=[whole()] * 3,
        out_shape=[jax.ShapeDtypeStruct(*s) for s in shapes],
        scratch_shapes=[
            pltpu.VMEM((2, TILE, MOST * TILE), F32),
            pltpu.VMEM((HEADS, 2, TILE, MOST * TILE), BF16),
            pltpu.VMEM((HEADS, 2, TILE, MOST * TILE), BF16),
            pltpu.VMEM((rows, width), F32),
            pltpu.VMEM((rows, width), BF16),
        ],
        compiler_params=pltpu.CompilerParams(vmem_limit_bytes=SCOPED),
        cost_estimate=pl.CostEstimate(
            flops=2 * 800 * MIB, bytes_accessed=16 * MIB, transcendentals=MIB
        ),
    )(lengths, proj, slope, near, near_slope, d_gated)


def key_grad_kernel(near_normed, normed, near_d_pre, d_pre, send, keep):
    width = normed.shape[1]
    even = lax.axis_index("core") == 0
    half = width // 2
    side, depth = keep.shape[:2]
    d_key = jnp.concatenate([near_d_pre[:, width:], d_pre[:, 3 * width :]], axis=0)
    upper = lax.broadcasted_iota(jnp.int32, (1, 8, half), 1) < 4
    step = width // depth
    for z in range(depth):
        at = slice(z * step, (z + 1) * step)
        part = jnp.concatenate([near_normed[:, at], normed[:, at]], axis=0)
        grad = dot_tn(part, d_key).reshape(side * side, 8, width)
        left, right = grad[:, :, :half], grad[:, :, half:]
        first = jnp.where(upper, left, pltpu.roll(right, 4, 1))
        last = jnp.where(upper, pltpu.roll(left, 4, 1), right)
        kept = jnp.where(even, first, last).astype(BF16)
        sent = jnp.where(even, last, first).astype(BF16)
        for y in range(side):
            keep[y, z] = kept[y * side : (y + 1) * side]
            send[y, z] = sent[y * side : (y + 1) * side]


def key_grad(near_normed, normed, near_d_pre, d_pre):
    width = normed.shape[1]
    depth, side = lax.axis_size("dp"), lax.axis_size("x")
    shape = jax.ShapeDtypeStruct((side, depth, side, 8, width // 2), BF16)
    return pl.pallas_call(
        key_grad_kernel,
        in_specs=[whole()] * 4,
        out_specs=[whole()] * 2,
        out_shape=[shape, shape],
        compiler_params=pltpu.CompilerParams(vmem_limit_bytes=SCOPED),
        cost_estimate=TINY,
    )(near_normed, normed, near_d_pre, d_pre)


def ring_first_kernel(keep, received, total, up, down):
    place = lax.axis_index("y")
    half = up.shape[0]
    total[...] = (keep[...].astype(F32) + received[...].astype(F32)).astype(BF16)
    opposite = total.at[lax.rem(place + 2, 4)]
    up[...] = opposite[:half]
    down[...] = opposite[half:]


def ring_second_kernel(total, from_below, from_above, up, down):
    place = lax.axis_index("y")
    half = from_below.shape[0]
    above, below = total.at[lax.rem(place + 1, 4)], total.at[lax.rem(place + 3, 4)]
    up[:half] = (above[:half].astype(F32) + from_below[...].astype(F32)).astype(BF16)
    up[half:] = above[half:]
    down[:half] = below[:half]
    down[half:] = (below[half:].astype(F32) + from_above[...].astype(F32)).astype(BF16)


def ring_third_kernel(total, from_below, from_above, column):
    own = total.at[lax.axis_index("y")]
    column[...] = (
        own[...].astype(F32) + from_below[...].astype(F32) + from_above[...].astype(F32)
    ).astype(BF16)


def on_device(kernel, shapes, *arrays):
    return pl.pallas_call(
        kernel,
        in_specs=[whole()] * len(arrays),
        out_specs=[whole()] * len(shapes),
        out_shape=[jax.ShapeDtypeStruct(shape, BF16) for shape in shapes],
        compiler_params=pltpu.CompilerParams(vmem_limit_bytes=SCOPED),
        cost_estimate=TINY,
    )(*arrays)


def near_through_kernel(near_d_pre, weight, far, out):
    width = weight.shape[0]
    step = 256
    for n in range(0, width, step):
        at = slice(n, n + step)
        near = dot_nt(near_d_pre[:, :width], weight[at, width : 2 * width])
        near = (near + dot_nt(near_d_pre[:, width:], weight[at, 3 * width :])).astype(BF16)
        far[:, at] = near[:TILE]
        out[:, at] = near[TILE:]


def near_through(near_d_pre, weight):
    halo, width = near_d_pre.shape[0], weight.shape[0]
    return pl.pallas_call(
        near_through_kernel,
        in_specs=[whole()] * 2,
        out_specs=[whole()] * 2,
        out_shape=[
            jax.ShapeDtypeStruct((TILE, width), BF16), jax.ShapeDtypeStruct((halo - TILE, width), BF16)
        ],
        compiler_params=pltpu.CompilerParams(vmem_limit_bytes=SCOPED),
        cost_estimate=TINY,
    )(near_d_pre, weight)


def through_kernel(d_pre, gated, mine, second, weight, weight_out, d_normed, outs):
    width = weight.shape[0]
    step = 256
    for n in range(0, width, step):
        at = slice(n, n + step)
        d_normed[:, at] = dot_nt(d_pre[...], weight[at, :])
        update = dot_nn(gated[...], weight_out[:, at])
        outs[:TILE, at] = (mine[:, at].astype(F32) + update[:TILE]).astype(BF16)
        outs[TILE:, at] = (second[:, at].astype(F32) + update[TILE:]).astype(BF16)


def through(d_pre, gated, mine, second, weight, weight_out):
    rows, width = d_pre.shape[0], weight.shape[0]
    return pl.pallas_call(
        through_kernel,
        in_specs=[whole()] * 6,
        out_specs=[whole()] * 2,
        out_shape=[
            jax.ShapeDtypeStruct((rows, width), F32), jax.ShapeDtypeStruct((rows, width), BF16)
        ],
        compiler_params=pltpu.CompilerParams(vmem_limit_bytes=SCOPED),
        cost_estimate=TINY,
    )(d_pre, gated, mine, second, weight, weight_out)


def merge_kernel(d_normed, arrived, outs, own, given):
    own[...] = d_normed[:TILE, :] + arrived[:TILE, :].astype(F32)
    given[:TILE, :] = outs[TILE:, :]
    given[TILE:, :] = (d_normed[TILE:, :] + arrived[TILE:, :].astype(F32)).astype(BF16)


def merge(d_normed, arrived, outs):
    rows, width = outs.shape
    return pl.pallas_call(
        merge_kernel,
        in_specs=[whole()] * 3,
        out_specs=[whole()] * 2,
        out_shape=[
            jax.ShapeDtypeStruct((TILE, width), F32),
            jax.ShapeDtypeStruct((rows, width), BF16),
        ],
        compiler_params=pltpu.CompilerParams(vmem_limit_bytes=SCOPED),
        cost_estimate=TINY,
    )(d_normed, arrived, outs)


def finish_kernel(
    events, back, outs, own, taken, far, layer_out, event_grads, layer, grads, sems
):
    core = lax.axis_index("core")
    kept = pl.ds(pl.multiple_of(core * TILE, TILE), TILE)
    swapped = pl.ds(pl.multiple_of((1 - core) * TILE, TILE), TILE)
    layer[0] = outs[:TILE, :]
    layer[1] = taken[:TILE, :]
    stores = [
        pltpu.make_async_copy(layer.at[r], layer_out.at[rows], sems.at[r])
        for r, rows in enumerate((kept, swapped))
    ]
    for copy in stores:
        copy.start()
    sums = (
        (kept, own[...]),
        (swapped, taken[TILE:, :].astype(F32) + far[...].astype(F32)),
    )
    for r, (rows, d_normed) in enumerate(sums):
        normed_f, recip = normalize(events[rows, :].astype(F32))
        grads[r] = (back[rows, :].astype(F32) + norm_back(d_normed, normed_f, recip)).astype(BF16)
        stores.append(pltpu.make_async_copy(grads.at[r], event_grads.at[rows], sems.at[2 + r]))
        stores[-1].start()
    for copy in stores:
        copy.wait()


def finish(events, back, outs, own, taken, far):
    rows, width = events.shape
    return pl.pallas_call(
        finish_kernel,
        in_specs=[whole()] * 6,
        out_specs=[remote()] * 2,
        out_shape=[jax.ShapeDtypeStruct((rows, width), BF16)] * 2,
        scratch_shapes=[
            pltpu.VMEM((2, TILE, width), BF16),
            pltpu.VMEM((2, TILE, width), BF16),
            pltpu.SemaphoreType.DMA((4,)),
        ],
        compiler_params=pltpu.CompilerParams(vmem_limit_bytes=SCOPED),
        cost_estimate=pl.CostEstimate(flops=4 * MIB, bytes_accessed=4 * MIB, transcendentals=0),
    )(events, back, outs, own, taken, far)


def sum_kernel(parts, out):
    total = parts[0].astype(F32)
    for n in range(1, parts.shape[0]):
        total = total + parts[n].astype(F32)
    out[:, : total.shape[1]] = total[:4]
    out[:, total.shape[1] :] = total[4:]


def sum_parts(parts):
    return pl.pallas_call(
        sum_kernel,
        in_specs=[whole()],
        out_specs=whole(),
        out_shape=jax.ShapeDtypeStruct((4, 2 * parts.shape[-1]), F32),
        compiler_params=pltpu.CompilerParams(vmem_limit_bytes=SCOPED),
        cost_estimate=TINY,
    )(parts)


def around(block, shift):
    return lax.ppermute(block, "y", [(i, (i + shift) % 4) for i in range(4)])


def shards(events, lengths, weight_in, weight_out, cotangent):
    pairs = lax.axis_size(SEQ)
    onward, far_on, backward, far_back = routes(pairs)
    swap = [(i, i ^ 1) for i in range(pairs)]
    local = events.reshape(2 * TILE, -1)
    back = cotangent.reshape(2 * TILE, -1)

    mine, other = split(local)
    far = move(other, far_on)
    second = move(other, swap)
    back_mine, back_other = split(back)
    back_second = move(back_other, swap)
    normed = normalize_block(mine, second)
    near = move(normed, onward)

    far, normed = lax.optimization_barrier((far, normed))
    proj, slope, d_gated = project(normed, back_mine, back_second, weight_in, weight_out)
    far, near, proj = lax.optimization_barrier((far, near, proj))
    near_normed, near, near_slope = project_near(far, near, weight_in)
    gated, d_pre, near_d_pre = attention(lengths, proj, slope, near, near_slope, d_gated)

    tie = lax.optimization_barrier
    far_d, near_d = near_through(near_d_pre, weight_in)
    arrived = move(near_d, backward)
    near_d_pre, near_d = tie((near_d_pre, near_d))
    send, keep = key_grad(near_normed, normed, near_d_pre, d_pre)
    received = move(send, swap)

    block = keep.shape[1:]
    half = (block[0] // 2,) + block[1:]
    total, up, down = on_device(ring_first_kernel, [keep.shape, half, half], keep, received)
    from_below, from_above = around(up, 1), around(down, -1)
    d_pre, total = tie((d_pre, total))
    far_in = move(far_d, far_back)
    d_normed, outs = through(d_pre, gated, mine, second, weight_in, weight_out)
    from_below, from_above, d_normed = tie((from_below, from_above, d_normed))
    up, down = on_device(ring_second_kernel, [block, block], total, from_below, from_above)
    from_below, from_above = around(up, 1), around(down, -1)
    d_normed, up, far_in = tie((d_normed, up, far_in))
    own, given = merge(d_normed, arrived, outs)
    taken = move(given, swap)
    from_below, from_above, taken = tie((from_below, from_above, taken))
    (column,) = on_device(ring_third_kernel, [block], total, from_below, from_above)
    column = column.reshape((block[0] * block[1],) + block[2:])
    parts = lax.all_to_all(column, ("dp", "x"), split_axis=0, concat_axis=0, tiled=True)
    layer_out, event_grads = finish(local, back, outs, own, taken, far_in)
    summed = sum_parts(parts)
    return (layer_out.reshape(events.shape), event_grads.reshape(events.shape), summed)


def solution(mesh):
    devices = mesh.devices
    fine = Mesh(devices.reshape(devices.shape[0], 4, 4, 2), ("dp",) + SEQ)
    every = P("dp", SEQ, None, None)
    return jax.shard_map(
        shards,
        mesh=fine,
        in_specs=(every, P("dp", None), P(), P(), every),
        out_specs=(every, every, P(("dp",) + SEQ, None)),
        check_vma=False,
    )
```
